128 devices in a mesh: row: 4 (over z_lo, core), col: 32 (over x, z_hi, y).
Axes of the slice: x: 4, y: 4, z: 4 (z_hi: 2, z_lo: 2; z = z_hi * 2 + z_lo), core: 2. Of those that a mesh axis runs over, the one named last changes fastest.
Arguments:
- visibilities: bfloat16 [32, 8, 1, 512, 512], P(None, None, None, 'col', 'row'), may hold values from -6 to 6
- coherencies: bfloat16 [32, 16, 8, 1, 512, 512], P(None, None, None, None, 'col', 'row'), may hold values from -1.1953125 to 1.1953125
- flags: int32 [32, 1, 512, 512], P(None, None, 'col', 'row'), may hold values 0 or 1
- freedom: int32 [512], replicated, may hold values from 2 to 12
- gains: float32 [32, 8, 16, 512], P(None, None, None, ('row', 'col')), may hold values from -4 to 4
Outputs:
- new_gains: float32 [32, 8, 16, 512], P(None, None, None, ('row', 'col'))
The draws below stay inside these ranges and needn't reach their ends.
All inputs are finite; a program needn't handle non-finite values. No bound on the sum of `flags` on one device may be relied on, other than what follows from the above.
Results may differ from the reference program's by a relative error of at most 0.0003.
Values sent between devices are 32-bit elements; how exact they have to be, the bound alone decides.
A program may use at most 192 MiB of HBM per device.

```python
import jax
import jax.numpy as jnp
from jax import lax

STATIONS = 512
DIRS = 16
CHANS = 32
SAMPLES = 1


def set_ends(array, own_key, smallest, high):
    spot = [jax.random.randint(jax.random.fold_in(own_key, axis), (), 0, length) for axis, length in enumerate(array.shape)]
    longest = array.shape.index(max(array.shape))
    beside = spot[:longest] + [(spot[longest] + 1) % array.shape[longest]] + spot[longest + 1:]
    return array.at[tuple(spot)].set(smallest).at[tuple(beside)].set(high)


def steps_of(own_key, shape, cuts, least, largest):
    factor_of = 1.0
    for position, shards_of in cuts:
        steps = jax.random.uniform(jax.random.fold_in(jax.random.fold_in(own_key, 6), position), (shards_of,), jnp.float32, least / len(cuts), largest / len(cuts))
        factor_of = factor_of * jnp.repeat(jnp.exp(steps), shape[position] // shards_of).reshape((-1,) + (1,) * (len(shape) - 1 - position))
    return factor_of


def scatter_about(rng, extent, width, most, cuts=(), kind=jnp.bfloat16):
    factor_of = steps_of(rng, extent, cuts, -0.22, 0.18) if cuts else 1.0
    drawn = jax.random.normal(rng, extent, jnp.float32) * width * factor_of
    return jnp.minimum(jnp.maximum(drawn, -most), most).astype(kind)


def setup_inputs(seed: int = 0) -> dict:
    seeds = jax.random.split(jax.random.key(seed), 6)
    visibilities = scatter_about(seeds[0], (CHANS, 8, SAMPLES, STATIONS, STATIONS), 1.0, 6.0, ((3, 32), (4, 4)))
    coherencies = scatter_about(seeds[1], (CHANS, DIRS, 8, SAMPLES, STATIONS, STATIONS), 0.2, 1.1953125, ((4, 32), (5, 4)))
    flags = set_ends((jax.random.randint(seeds[2], (CHANS, SAMPLES, STATIONS, STATIONS), 0, 8) < 7).astype(jnp.int32), jax.random.fold_in(seeds[2], 1), 0, 1)
    freedom = set_ends(jax.random.randint(seeds[3], (STATIONS,), 2, 13), jax.random.fold_in(seeds[3], 1), 2, 12).astype(jnp.int32)
    gains = scatter_about(seeds[4], (CHANS, 8, DIRS, STATIONS), 0.7, 4.0, ((3, 128),), jnp.float32)
    return dict(visibilities=visibilities, coherencies=coherencies, flags=flags, freedom=freedom, gains=gains)


damping = 1.0


def product(a, b):
    out = [None] * 8
    for i in range(2):
        for j in range(2):
            real = a[2 * i] * b[j] - a[4 + 2 * i] * b[4 + j] + a[2 * i + 1] * b[2 + j] - a[5 + 2 * i] * b[6 + j]
            imag = a[2 * i] * b[4 + j] + a[4 + 2 * i] * b[j] + a[2 * i + 1] * b[6 + j] + a[5 + 2 * i] * b[2 + j]
            out[2 * i + j] = real
            out[4 + 2 * i + j] = imag
    return out


def adjoint(a):
    out = [None] * 8
    for i in range(2):
        for j in range(2):
            out[2 * i + j] = a[2 * j + i]
            out[4 + 2 * i + j] = -a[4 + 2 * j + i]
    return out


def update(own, share):
    numer = [share[m] for m in range(8)]
    upper_a = share[8] + damping
    lower_d = share[9] + damping
    part_re = share[10]
    part_im = share[11]
    determ = upper_a * lower_d - part_re * part_re - part_im * part_im
    zeros = jnp.zeros_like(upper_a)
    inverse = [lower_d / determ, -part_re / determ, -part_re / determ, upper_a / determ,
               zeros, -part_im / determ, part_im / determ, zeros]
    step = product(numer, inverse)
    return own + jnp.stack(step)


def reference(visibilities, coherencies, flags, freedom, gains):
    degree = freedom.astype(jnp.float32)
    nu_pair = degree[:, None] + degree[None, :]

    def channel(pieces):
        vis_c, coh_c, flag_c, gain_c = pieces

        def factors(k):
            coh_k = coh_c[k].astype(jnp.float32)
            gain_k = gain_c[:, k, :]
            coh_list = [coh_k[m] for m in range(8)]
            gain_q = [gain_k[m][None, :, None] for m in range(8)]
            gain_p = [gain_k[m][None, None, :] for m in range(8)]
            return product(coh_list, adjoint(gain_q)), gain_p

        def add_model(total, k):
            ylist, gain_p = factors(k)
            return total + jnp.stack(product(gain_p, ylist)), None

        start = jnp.zeros(vis_c.shape, jnp.float32)
        model, _ = lax.scan(add_model, start, jnp.arange(DIRS))
        resid = vis_c.astype(jnp.float32) - model
        energy = jnp.sum(resid * resid, axis=0)
        weight = flag_c.astype(jnp.float32) * (nu_pair + 8.0) / (nu_pair + energy)
        wres = [weight * resid[m] for m in range(8)]

        def terms(carry, k):
            ylist, _ = factors(k)
            numer = product(wres, adjoint(ylist))
            upper_a = weight * (ylist[0] ** 2 + ylist[4] ** 2 + ylist[1] ** 2 + ylist[5] ** 2)
            lower_d = weight * (ylist[2] ** 2 + ylist[6] ** 2 + ylist[3] ** 2 + ylist[7] ** 2)
            part_re = weight * (ylist[0] * ylist[2] + ylist[4] * ylist[6] + ylist[1] * ylist[3] + ylist[5] * ylist[7])
            part_im = weight * (ylist[4] * ylist[2] - ylist[0] * ylist[6] + ylist[5] * ylist[3] - ylist[1] * ylist[7])
            every = numer + [upper_a, lower_d, part_re, part_im]
            return carry, jnp.stack([jnp.sum(x, axis=(0, 1)) for x in every])

        _, sums = lax.scan(terms, jnp.float32(0.0), jnp.arange(DIRS))
        share = jnp.transpose(sums, (1, 0, 2))
        return update(gain_c, share)

    return lax.map(channel, (visibilities, coherencies, flags, gains))
```

```python
import jax
import jax.numpy as jnp
from jax import lax
from jax.experimental import pallas as pl
from jax.experimental.pallas import tpu as pltpu
from jax.sharding import PartitionSpec as P

F32 = jnp.float32
BF16 = jnp.bfloat16
MESH = pl.DeviceIdType.MESH
damping = 1.0


def product(a, b):
    out = [None] * 8
    for i in range(2):
        for j in range(2):
            real = (
                a[2 * i] * b[j]
                - a[4 + 2 * i] * b[4 + j]
                + a[2 * i + 1] * b[2 + j]
                - a[5 + 2 * i] * b[6 + j]
            )
            imag = (
                a[2 * i] * b[4 + j]
                + a[4 + 2 * i] * b[j]
                + a[2 * i + 1] * b[6 + j]
                + a[5 + 2 * i] * b[2 + j]
            )
            out[2 * i + j] = real
            out[4 + 2 * i + j] = imag
    return out


def prepare_gains(g, gq, gv, tab):
    a = g[:64]
    b = g[64:]
    gv[0] = a
    gv[1] = a + b
    gv[2] = b - a
    r = jnp.concatenate([gq] * 8, axis=0).T
    lane = lax.broadcasted_iota(jnp.int32, (16, 128), 1)
    sec = (lane // 16) % 4
    low = lane >= 64

    def pick(u0, u1, u2, u3):
        return jnp.where(sec == 0, u0, jnp.where(sec == 1, u1, jnp.where(sec == 2, u2, u3)))

    for j in range(2):
        r0, r1, i0, i1 = (r[m * 16 : m * 16 + 16] for m in (2 * j, 2 * j + 1, 4 + 2 * j, 5 + 2 * j))
        rows = [pick(r0, r1, i0, i1), pick(-i0, -i1, r0, r1), pick(r0 - i0, r1 - i1, i0 + r0, i1 + r1)]
        for v in range(3):
            hi = rows[v].astype(BF16).astype(F32)
            tab[j * 3 + v] = jnp.where(low, rows[v] - hi, hi)


def channel_sums(coh, vis, flag, nu, gv, tab, ys, wr, red, slab):
    lane = lax.broadcasted_iota(jnp.int32, (16, 128), 1)
    line = lax.broadcasted_iota(jnp.int32, (16, 128), 0)
    diag = (lane % 16) == line
    acc = [[jnp.zeros((16, 128), F32) for _ in range(3)] for _ in range(4)]
    for k in range(16):
        lhs = jnp.concatenate([jnp.where(diag, tab[g, k : k + 1, :], 0.0) for g in range(6)], axis=0).astype(BF16)
        half = jnp.concatenate(
            [
                jnp.concatenate([coh[k, 4 * ri + l], coh[k, 4 * ri + 2 + l]], axis=1)
                for ri in range(2)
                for l in range(2)
            ],
            axis=0,
        )
        out = jnp.dot(lhs, jnp.concatenate([half, half], axis=0), preferred_element_type=F32)
        y = {}
        for i in range(2):
            for j in range(2):
                for v in range(3):
                    t = out[(j * 3 + v) * 16 : (j * 3 + v) * 16 + 16, i * 128 : i * 128 + 128]
                    y[i, j, v] = t
                    ys[k, (i * 2 + j) * 3 + v] = t
        for i in range(2):
            for j in range(2):
                for l in range(2):
                    at = (2 * i + l) * 16 + k
                    ga, gs, gd = (gv[v, at : at + 1, :] for v in range(3))
                    part = acc[2 * i + j]
                    part[0] = part[0] + ga * y[l, j, 2]
                    part[1] = part[1] + gs * y[l, j, 1]
                    part[2] = part[2] + gd * y[l, j, 0]
    resid = []
    energy = None
    for m in range(4):
        re = vis[m].astype(F32) - (acc[m][0] - acc[m][1])
        im = vis[4 + m].astype(F32) - (acc[m][0] + acc[m][2])
        resid.append((re, im))
        t = re * re + im * im
        energy = t if energy is None else energy + t
    w = flag.astype(F32) * (nu + 8.0) / (nu + energy)
    for m in range(4):
        a = w * resid[m][0]
        b = w * resid[m][1]
        wr[m * 3] = a
        wr[m * 3 + 1] = a - b
        wr[m * 3 + 2] = a + b
    wr[12] = w
    for k in range(16):
        tot = [None] * 12
        cross = [[None] * 3 for _ in range(4)]
        for h in range(2):
            s = slice(8 * h, 8 * h + 8)
            y = [[[ys[k, (i * 2 + j) * 3 + v, s] for v in range(3)] for j in range(2)] for i in range(2)]
            for i in range(2):
                for j in range(2):
                    for l in range(2):
                        yr, yi, both = y[j][l]
                        at = (2 * i + l) * 3
                        terms = (wr[at, s] * both, wr[at + 1, s] * yi, wr[at + 2, s] * yr)
                        part = cross[2 * i + j]
                        for v in range(3):
                            part[v] = terms[v] if part[v] is None else part[v] + terms[v]
            (r00, i00, _), (r01, i01, _) = y[0]
            (r10, i10, _), (r11, i11, _) = y[1]
            every = (
                r00 * r00 + i00 * i00 + r01 * r01 + i01 * i01,
                r10 * r10 + i10 * i10 + r11 * r11 + i11 * i11,
                r00 * r10 + i00 * i10 + r01 * r11 + i01 * i11,
                i00 * r10 - r00 * i10 + i01 * r11 - r01 * i11,
            )
            for t in range(4):
                x = wr[12, s] * every[t]
                tot[8 + t] = x if h == 0 else tot[8 + t] + x
        for m in range(4):
            tot[m] = cross[m][0] - cross[m][1]
            tot[4 + m] = cross[m][2] - cross[m][0]
        for t in range(12):
            red[pl.ds((t * 16 + k) * 8, 8), :] = tot[t]
    for b in range(24):
        s = None
        for j in range(8):
            x = red[pl.ds(b * 64 + j, 8, stride=8), :]
            s = x if s is None else s + x
        slab[pl.ds(b * 8, 8), :] = s


def updated(g, total):
    share = [total[t * 16 : t * 16 + 16] for t in range(12)]
    upper_a = share[8] + damping
    lower_d = share[9] + damping
    part_re = share[10]
    part_im = share[11]
    determ = upper_a * lower_d - part_re * part_re - part_im * part_im
    zeros = jnp.zeros_like(upper_a)
    inverse = [
        lower_d / determ,
        -part_re / determ,
        -part_re / determ,
        upper_a / determ,
        zeros,
        -part_im / determ,
        part_im / determ,
        zeros,
    ]
    return g + jnp.concatenate(product(share[:8], inverse), axis=0)


def kernel(
    vis_hbm, coh_hbm, flag_hbm, free_ref, own_ref, fin,
    coh_v, vis_v, flag_v, ag, gqb, gv, tab, ys, wr, red, nu_v, gsv,
    slabs, r1, p1, r2, p2, r3, fsrc, f1,
    load_sem, s1_send, s1_recv, gq_send, gq_recv, s3_send, s3_recv,
    p1_send, p1_recv, p2_send, p2_recv, p3_send, p3_recv, f1_send, f1_recv, f2_send, f2_recv,
):
    row = lax.axis_index("row")
    col = lax.axis_index("col")
    x = col // 8
    z = (col // 4) % 2
    y = col % 4

    def col_of(xx, zz, yy):
        return xx * 8 + zz * 4 + yy

    def moved(t, da, dz, db):
        return col_of((x + (1 - t) * da + t * db) % 4, (z + dz) % 2, (y + t * da + (1 - t) * db) % 4)

    def axis_a(t):
        return x + t * (y - x)

    def axis_b(t):
        return y + t * (x - y)

    def step(n):
        t = n % 2
        s = (n // 2 + 1) % 4
        g = (n // 8 + 1) % 4
        alpha = (axis_a(t) + s) % 4
        beta = (axis_b(t) + g) % 4
        return t, g, s, alpha, beta

    def channel_of(t, alpha, beta):
        return (1 - t) * (alpha * 8 + beta) + t * (beta * 8 + 4 + alpha)

    def load(n):
        t, _, _, alpha, beta = step(n)
        return pltpu.make_async_copy(coh_hbm.at[channel_of(t, alpha, beta)], coh_v.at[n], load_sem.at[n])

    vis_copy = pltpu.make_async_copy(vis_hbm, vis_v, load_sem.at[32])
    flag_copy = pltpu.make_async_copy(flag_hbm, flag_v, load_sem.at[33])

    gq_row = x
    gq_cols = [col_of(z * 2 + y // 2, y % 2, m) for m in range(4)]
    gq_target = col_of(row, x // 2, (x % 2) * 2 + z)
    gq_here = [jnp.logical_and(gq_row == row, gq_cols[m] == col) for m in range(4)]
    gq_self = [jnp.logical_and(gq_target == col, row == r) for r in range(4)]
    is_self = (gq_target == col).astype(jnp.int32)

    peers = [moved(0, da, 0, 0) for da in (1, 2, 3)]
    peers += [moved(0, 0, dz, db) for dz in range(2) for db in range(4) if (dz, db) != (0, 0)]
    peers += [moved(0, da, 1, 0) for da in (1, 2, 3)]
    barrier = pltpu.get_barrier_semaphore()
    for peer in peers:
        pl.semaphore_signal(barrier, inc=1, device_id=(row, peer), device_id_type=MESH)
    for m in range(4):
        @pl.when(jnp.logical_not(gq_here[m]))
        def _():
            pl.semaphore_signal(barrier, inc=1, device_id=(gq_row, gq_cols[m]), device_id_type=MESH)

    lax.fori_loop(0, 2, lambda n, u: (load(n).start(), u)[1], 0)
    vis_copy.start()
    flag_copy.start()
    lax.fori_loop(2, 32, lambda n, u: (load(n).start(), u)[1], 0)

    for t in range(2):
        ag[t, :, :, axis_a(t), z, axis_b(t)] = own_ref[t]
    for m in range(4):
        @pl.when(gq_here[m])
        def _():
            for t in range(2):
                gqb[t, :, :, m] = own_ref[t]

    lane = lax.broadcasted_iota(jnp.int32, (16, 128), 1)
    line = lax.broadcasted_iota(jnp.int32, (16, 128), 0)
    free_q = jnp.broadcast_to(free_ref[pl.ds(x, 1), :].astype(F32), (16, 128))
    free_q = jnp.sum(jnp.where(lane == (z * 4 + y) * 16 + line, free_q, 0.0), axis=1, keepdims=True)
    nu_v[...] = free_q + free_ref[pl.ds(row, 1), :].astype(F32)

    pl.semaphore_wait(barrier, 17 - is_self)

    def s1(t, dz, db):
        at = t * 8 + dz * 4 + db
        return pltpu.make_async_remote_copy(
            src_ref=own_ref.at[t],
            dst_ref=ag.at[t, :, :, axis_a(t), z, axis_b(t)],
            send_sem=s1_send.at[at],
            recv_sem=s1_recv.at[at],
            device_id=(row, moved(t, 0, dz, db)),
            device_id_type=MESH,
        )

    def gq_copy(t, r):
        return pltpu.make_async_remote_copy(
            src_ref=own_ref.at[t],
            dst_ref=gqb.at[t, :, :, y],
            send_sem=gq_send.at[t * 4 + r],
            recv_sem=gq_recv.at[t * 4 + y],
            device_id=(r, gq_target),
            device_id_type=MESH,
        )

    def gq_arrival(t, m):
        return pltpu.make_async_remote_copy(
            src_ref=own_ref.at[t],
            dst_ref=gqb.at[t, :, :, m],
            send_sem=gq_send.at[t * 4],
            recv_sem=gq_recv.at[t * 4 + m],
            device_id=(gq_row, gq_cols[m]),
            device_id_type=MESH,
        )

    plane = [(dz, db) for dz in range(2) for db in range(4) if (dz, db) != (0, 0)]
    for dz, db in plane:
        for t in range(2):
            s1(t, dz, db).start()
    for r in range(4):
        @pl.when(jnp.logical_not(gq_self[r]))
        def _():
            for t in range(2):
                gq_copy(t, r).start()

    def s3(t, g, s):
        at = t * 16 + g * 4 + s
        block = ag.at[t, (axis_b(t) + g) % 4, :, axis_a(t)]
        return pltpu.make_async_remote_copy(
            src_ref=block,
            dst_ref=block,
            send_sem=s3_send.at[at],
            recv_sem=s3_recv.at[at],
            device_id=(row, moved(t, s, 0, 0)),
            device_id_type=MESH,
        )

    for t in range(2):
        for dz, db in plane:
            s1(t, dz, db).wait_recv()
    for g in (1, 2, 3, 0):
        for t in range(2):
            for s in (1, 2, 3):
                s3(t, g, s).start()
    for m in range(4):
        @pl.when(jnp.logical_not(gq_here[m]))
        def _():
            for t in range(2):
                gq_arrival(t, m).wait_recv()
    vis_copy.wait()
    flag_copy.wait()

    def send1(n):
        t, g, s, _, _ = step(n)
        at = t * 16 + g * 4 + s
        return pltpu.make_async_remote_copy(
            src_ref=slabs.at[n],
            dst_ref=r1.at[t, g, s - 1],
            send_sem=p1_send.at[at],
            recv_sem=p1_recv.at[at],
            device_id=(row, moved(t, s, 0, 0)),
            device_id_type=MESH,
        )

    def send2(t, g):
        at = t * 4 + g
        return pltpu.make_async_remote_copy(
            src_ref=p1.at[t, g],
            dst_ref=r2.at[t, g - 1],
            send_sem=p2_send.at[at],
            recv_sem=p2_recv.at[at],
            device_id=(row, moved(t, 0, 0, g)),
            device_id_type=MESH,
        )

    send3 = pltpu.make_async_remote_copy(
        src_ref=p2.at[1 - z],
        dst_ref=r3,
        send_sem=p3_send,
        recv_sem=p3_recv,
        device_id=(row, moved(0, 0, 1, 0)),
        device_id_type=MESH,
    )

    def sum1(t, gi):
        g = (gi + 1) % 4
        for i in range(3):
            send1(gi * 8 + 2 * i + t).wait_recv()
        p1[t, g] = slabs[gi * 8 + 6 + t] + r1[t, g, 0] + r1[t, g, 1] + r1[t, g, 2]

    def body(n, carry):
        t, g, s, alpha, beta = step(n)
        load(n).wait()

        @pl.when(s == 1)
        def _():
            for i in (1, 2, 3):
                s3(t, g, i).wait_recv()

        pieces = []
        for xx in range(4):
            for zz in range(2):
                for yy in range(4):
                    pieces.append(ag[t, beta, alpha, xx + t * (yy - xx), zz, yy + t * (xx - yy)])
        gains = jnp.concatenate(pieces, axis=0).T
        gq = jnp.concatenate([gqb[t, beta, alpha, m] for m in range(4)], axis=0)
        prepare_gains(gains, gq, gv, tab)

        @pl.when(n >= 30)
        def _():
            gsv[t] = gains

        c = channel_of(t, alpha, beta)
        channel_sums(
            coh_v.at[n], vis_v.at[c], flag_v[c], nu_v[...], gv, tab, ys, wr, red, slabs.at[n]
        )

        @pl.when(s != 0)
        def _():
            send1(n).start()

        @pl.when(jnp.logical_and(s == 2, n >= 8))
        def _():
            sum1(t, n // 8 - 1)
            send2(t, n // 8).start()

        return carry

    lax.fori_loop(0, 32, body, 0)

    for t in range(2):
        sum1(t, 3)
        for g in (1, 2, 3):
            send2(t, g).wait_recv()
        p2[t] = p1[t, 0] + r2[t, 0] + r2[t, 1] + r2[t, 2]
    send3.start()
    send3.wait_recv()
    fresh = updated(gsv[z], p2[z] + r3[...]).T
    for d in range(32):
        fsrc[d] = fresh[d * 4 : d * 4 + 4]

    def f1_copy(dx):
        return pltpu.make_async_remote_copy(
            src_ref=fsrc.at[pl.ds(((x + dx) % 4) * 8, 8)],
            dst_ref=f1.at[x],
            send_sem=f1_send.at[dx],
            recv_sem=f1_recv.at[dx],
            device_id=(row, moved(0, dx, 0, 0)),
            device_id_type=MESH,
        )

    def f2_copy(dz, dy):
        zz = (z + dz) % 2
        yy = (y + dy) % 4
        return pltpu.make_async_remote_copy(
            src_ref=f1.at[:, zz * 4 + yy],
            dst_ref=fin.at[:, z * 4 + y],
            send_sem=f2_send.at[dz * 4 + dy],
            recv_sem=f2_recv.at[dz * 4 + dy],
            device_id=(row, moved(0, 0, dz, dy)),
            device_id_type=MESH,
        )

    for dx in (1, 2, 3):
        f1_copy(dx).start()
    f1[x] = fsrc[pl.ds(x * 8, 8)]
    for dx in (1, 2, 3):
        f1_copy(dx).wait_recv()
    for dz, dy in plane:
        f2_copy(dz, dy).start()
    fin[:, z * 4 + y] = f1[:, z * 4 + y]
    for dz, dy in plane:
        f2_copy(dz, dy).wait_recv()

    for t in range(2):
        for dz, db in plane:
            s1(t, dz, db).wait_send()
    for r in range(4):
        @pl.when(jnp.logical_not(gq_self[r]))
        def _():
            for t in range(2):
                gq_copy(t, r).wait_send()
    for g in range(4):
        for t in range(2):
            for s in (1, 2, 3):
                s3(t, g, s).wait_send()

    def drain(n, carry):
        @pl.when((n // 2 + 1) % 4 != 0)
        def _():
            send1(n).wait_send()
        return carry

    lax.fori_loop(0, 32, drain, 0)
    for t in range(2):
        for g in (1, 2, 3):
            send2(t, g).wait_send()
    send3.wait_send()
    for dx in (1, 2, 3):
        f1_copy(dx).wait_send()
    for dz, dy in plane:
        f2_copy(dz, dy).wait_send()


def per_device(visibilities, coherencies, flags, freedom, gains):
    parts = jnp.transpose(gains.reshape(4, 2, 4, 128, 4), (1, 0, 2, 4, 3))
    own = jnp.stack([jnp.transpose(parts[0], (1, 0, 2, 3)), parts[1]])
    vmem = pl.BlockSpec(memory_space=pltpu.VMEM)
    hbm = pl.BlockSpec(memory_space=pl.ANY)
    dma = pltpu.SemaphoreType.DMA
    slab = (192, 128)
    fin = pl.pallas_call(
        kernel,
        out_shape=jax.ShapeDtypeStruct((4, 8, 4, 128), F32),
        in_specs=[hbm, hbm, hbm, vmem, vmem],
        out_specs=vmem,
        scratch_shapes=[
            pltpu.VMEM((32, 16, 8, 16, 128), BF16),
            pltpu.VMEM((32, 8, 16, 128), BF16),
            pltpu.VMEM((32, 16, 128), jnp.int32),
            pltpu.VMEM((2, 4, 4, 4, 2, 4, 4, 128), F32),
            pltpu.VMEM((2, 4, 4, 4, 4, 128), F32),
            pltpu.VMEM((3, 64, 128), F32),
            pltpu.VMEM((6, 16, 128), F32),
            pltpu.VMEM((16, 12, 16, 128), F32),
            pltpu.VMEM((13, 16, 128), F32),
            pltpu.VMEM((1536, 128), F32),
            pltpu.VMEM((16, 128), F32),
            pltpu.VMEM((2, 128, 128), F32),
            pltpu.VMEM((32,) + slab, F32),
            pltpu.VMEM((2, 4, 3) + slab, F32),
            pltpu.VMEM((2, 4) + slab, F32),
            pltpu.VMEM((2, 3) + slab, F32),
            pltpu.VMEM((2,) + slab, F32),
            pltpu.VMEM(slab, F32),
            pltpu.VMEM((32, 4, 128), F32),
            pltpu.VMEM((4, 8, 4, 128), F32),
            dma((34,)),
            dma((16,)), dma((16,)),
            dma((8,)), dma((8,)),
            dma((32,)), dma((32,)),
            dma((32,)), dma((32,)),
            dma((8,)), dma((8,)),
            dma, dma,
            dma((4,)), dma((4,)),
            dma((8,)), dma((8,)),
        ],
        compiler_params=pltpu.CompilerParams(
            collective_id=0, has_side_effects=True, vmem_limit_bytes=56 * 2**20
        ),
        cost_estimate=pl.CostEstimate(flops=10**9, bytes_accessed=2 * 10**7, transcendentals=0),
    )(
        visibilities.reshape(32, 8, 16, 128),
        coherencies.reshape(32, 16, 8, 16, 128),
        flags.reshape(32, 16, 128),
        freedom.reshape(4, 128),
        own,
    )
    return jnp.transpose(fin.reshape(32, 4, 8, 16), (0, 2, 3, 1))


def solution(mesh):
    return jax.shard_map(
        per_device,
        mesh=mesh,
        in_specs=(
            P(None, None, None, "col", "row"),
            P(None, None, None, None, "col", "row"),
            P(None, None, "col", "row"),
            P(),
            P(None, None, None, ("row", "col")),
        ),
        out_specs=P(None, None, None, ("row", "col")),
        check_vma=False,
    )
```

```python
import jax
import jax.numpy as jnp
from jax import lax
from jax.experimental import pallas as pl
from jax.experimental.pallas import tpu as pltpu
from jax.sharding import PartitionSpec as P

F32 = jnp.float32
BF16 = jnp.bfloat16
MESH = pl.DeviceIdType.MESH
damping = 1.0


def product(a, b):
    out = [None] * 8
    for i in range(2):
        for j in range(2):
            real = (
                a[2 * i] * b[j]
                - a[4 + 2 * i] * b[4 + j]
                + a[2 * i + 1] * b[2 + j]
                - a[5 + 2 * i] * b[6 + j]
            )
            imag = (
                a[2 * i] * b[4 + j]
                + a[4 + 2 * i] * b[j]
                + a[2 * i + 1] * b[6 + j]
                + a[5 + 2 * i] * b[2 + j]
            )
            out[2 * i + j] = real
            out[4 + 2 * i + j] = imag
    return out


def prepare_gains(g, gq, gv, tab):
    a = g[:64]
    b = g[64:]
    gv[0] = a
    gv[1] = a + b
    gv[2] = b - a
    r = jnp.concatenate([gq] * 8, axis=0).T
    lane = lax.broadcasted_iota(jnp.int32, (16, 128), 1)
    sec = (lane // 16) % 4
    low = lane >= 64

    def pick(u0, u1, u2, u3):
        return jnp.where(sec == 0, u0, jnp.where(sec == 1, u1, jnp.where(sec == 2, u2, u3)))

    for j in range(2):
        r0, r1, i0, i1 = (r[m * 16 : m * 16 + 16] for m in (2 * j, 2 * j + 1, 4 + 2 * j, 5 + 2 * j))
        rows = [pick(r0, r1, i0, i1), pick(-i0, -i1, r0, r1), pick(r0 - i0, r1 - i1, i0 + r0, i1 + r1)]
        for v in range(3):
            hi = rows[v].astype(BF16).astype(F32)
            tab[j * 3 + v] = jnp.where(low, rows[v] - hi, hi)


def channel_sums(coh, vis, flag, nu, gv, tab, ys, wr, red, slab):
    lane = lax.broadcasted_iota(jnp.int32, (16, 128), 1)
    line = lax.broadcasted_iota(jnp.int32, (16, 128), 0)
    diag = (lane % 16) == line
    acc = [[jnp.zeros((16, 128), F32) for _ in range(3)] for _ in range(4)]
    for k in range(16):
        lhs = jnp.concatenate([jnp.where(diag, tab[g, k : k + 1, :], 0.0) for g in range(6)], axis=0).astype(BF16)
        half = jnp.concatenate(
            [
                jnp.concatenate([coh[k, 4 * ri + l], coh[k, 4 * ri + 2 + l]], axis=1)
                for ri in range(2)
                for l in range(2)
            ],
            axis=0,
        )
        out = jnp.dot(lhs, jnp.concatenate([half, half], axis=0), preferred_element_type=F32)
        y = {}
        for i in range(2):
            for j in range(2):
                for v in range(3):
                    t = out[(j * 3 + v) * 16 : (j * 3 + v) * 16 + 16, i * 128 : i * 128 + 128]
                    y[i, j, v] = t
                    ys[k, (i * 2 + j) * 3 + v] = t
        for i in range(2):
            for j in range(2):
                for l in range(2):
                    at = (2 * i + l) * 16 + k
                    ga, gs, gd = (gv[v, at : at + 1, :] for v in range(3))
                    part = acc[2 * i + j]
                    part[0] = part[0] + ga * y[l, j, 2]
                    part[1] = part[1] + gs * y[l, j, 1]
                    part[2] = part[2] + gd * y[l, j, 0]
    resid = []
    energy = None
    for m in range(4):
        re = vis[m].astype(F32) - (acc[m][0] - acc[m][1])
        im = vis[4 + m].astype(F32) - (acc[m][0] + acc[m][2])
        resid.append((re, im))
        t = re * re + im * im
        energy = t if energy is None else energy + t
    w = flag.astype(F32) * (nu + 8.0) / (nu + energy)
    for m in range(4):
        a = w * resid[m][0]
        b = w * resid[m][1]
        wr[m * 3] = a
        wr[m * 3 + 1] = a - b
        wr[m * 3 + 2] = a + b
    wr[12] = w
    for k in range(16):
        tot = [None] * 12
        cross = [[None] * 3 for _ in range(4)]
        for h in range(2):
            s = slice(8 * h, 8 * h + 8)
            y = [[[ys[k, (i * 2 + j) * 3 + v, s] for v in range(3)] for j in range(2)] for i in range(2)]
            for i in range(2):
                for j in range(2):
                    for l in range(2):
                        yr, yi, both = y[j][l]
                        at = (2 * i + l) * 3
                        terms = (wr[at, s] * both, wr[at + 1, s] * yi, wr[at + 2, s] * yr)
                        part = cross[2 * i + j]
                        for v in range(3):
                            part[v] = terms[v] if part[v] is None else part[v] + terms[v]
            (r00, i00, _), (r01, i01, _) = y[0]
            (r10, i10, _), (r11, i11, _) = y[1]
            every = (
                r00 * r00 + i00 * i00 + r01 * r01 + i01 * i01,
                r10 * r10 + i10 * i10 + r11 * r11 + i11 * i11,
                r00 * r10 + i00 * i10 + r01 * r11 + i01 * i11,
                i00 * r10 - r00 * i10 + i01 * r11 - r01 * i11,
            )
            for t in range(4):
                x = wr[12, s] * every[t]
                tot[8 + t] = x if h == 0 else tot[8 + t] + x
        for m in range(4):
            tot[m] = cross[m][0] - cross[m][1]
            tot[4 + m] = cross[m][2] - cross[m][0]
        for t in range(12):
            red[pl.ds((t * 16 + k) * 8, 8), :] = tot[t]
    for b in range(24):
        s = None
        for j in range(8):
            x = red[pl.ds(b * 64 + j, 8, stride=8), :]
            s = x if s is None else s + x
        slab[pl.ds(b * 8, 8), :] = s


def updated(g, total):
    share = [total[t * 16 : t * 16 + 16] for t in range(12)]
    upper_a = share[8] + damping
    lower_d = share[9] + damping
    part_re = share[10]
    part_im = share[11]
    determ = upper_a * lower_d - part_re * part_re - part_im * part_im
    zeros = jnp.zeros_like(upper_a)
    inverse = [
        lower_d / determ,
        -part_re / determ,
        -part_re / determ,
        upper_a / determ,
        zeros,
        -part_im / determ,
        part_im / determ,
        zeros,
    ]
    return g + jnp.concatenate(product(share[:8], inverse), axis=0)


def kernel(
    vis_hbm, coh_hbm, flag_hbm, free_ref, own_ref, fin,
    coh_v, vis_v, flag_v, ag, gqb, gv, tab, ys, wr, red, nu_v, gsv,
    slabs, r1, p1, r2, p2, r3, fsrc, f1,
    gl, load_sem, s1_send, s1_recv, gq_send, gq_recv, s3_send, s3_recv,
    p1_send, p1_recv, p2_send, p2_recv, p3_send, p3_recv, f1_send, f1_recv, f2_send, f2_recv,
):
    row = lax.axis_index("row")
    col = lax.axis_index("col")
    x = col // 8
    z = (col // 4) % 2
    y = col % 4

    def col_of(xx, zz, yy):
        return xx * 8 + zz * 4 + yy

    def moved(t, da, dz, db):
        return col_of((x + (1 - t) * da + t * db) % 4, (z + dz) % 2, (y + t * da + (1 - t) * db) % 4)

    def axis_a(t):
        return x + t * (y - x)

    def axis_b(t):
        return y + t * (x - y)

    def step(n):
        t = n % 2
        s = (n // 2 + 1) % 4
        g = (n // 8 + 1) % 4
        alpha = (axis_a(t) + s) % 4
        beta = (axis_b(t) + g) % 4
        return t, g, s, alpha, beta

    def channel_of(t, alpha, beta):
        return (1 - t) * (alpha * 8 + beta) + t * (beta * 8 + 4 + alpha)

    def load(n):
        t, _, _, alpha, beta = step(n)
        return pltpu.make_async_copy(coh_hbm.at[channel_of(t, alpha, beta)], coh_v.at[n], load_sem.at[n])

    vis_copy = pltpu.make_async_copy(vis_hbm, vis_v, load_sem.at[32])
    flag_copy = pltpu.make_async_copy(flag_hbm, flag_v, load_sem.at[33])

    gq_target = (y, col_of(row, x // 2, (x % 2) * 2 + z))
    gq_source = (x, col_of(z * 2 + y // 2, y % 2, row))
    gq_far = jnp.logical_or(gq_target[0] != row, gq_target[1] != col)
    gq_from_far = jnp.logical_or(gq_source[0] != row, gq_source[1] != col)

    peers = [moved(0, da, 0, 0) for da in (1, 2, 3)]
    peers += [moved(0, 0, dz, db) for dz in range(2) for db in range(4) if (dz, db) != (0, 0)]
    peers += [moved(0, da, 1, 0) for da in (1, 2, 3)]
    barrier = pltpu.get_barrier_semaphore()
    for peer in peers:
        pl.semaphore_signal(barrier, inc=1, device_id=(row, peer), device_id_type=MESH)
    for dr in (1, 2, 3):
        pl.semaphore_signal(barrier, inc=1, device_id=((row + dr) % 4, col), device_id_type=MESH)

    @pl.when(gq_from_far)
    def _():
        pl.semaphore_signal(barrier, inc=1, device_id=gq_source, device_id_type=MESH)

    lax.fori_loop(0, 2, lambda n, u: (load(n).start(), u)[1], 0)
    vis_copy.start()
    flag_copy.start()
    lax.fori_loop(2, 32, lambda n, u: (load(n).start(), u)[1], 0)

    turned = jnp.concatenate([own_ref[:, p, :] for p in range(4)], axis=1).T
    for p in range(4):
        for cx in range(4):
            for cy in range(4):
                for t, beta, alpha in ((0, cy, cx), (1, cx, cy)):
                    at = p * 32 + cx * 8 + t * 4 + cy
                    gl[t, beta, alpha, p : p + 1] = turned[at : at + 1]
    for t in range(2):
        ag[t, :, :, x, z, y] = gl[t]

    @pl.when(jnp.logical_not(gq_from_far))
    def _():
        for t in range(2):
            gqb[t, :, :, row] = gl[t]

    lane = lax.broadcasted_iota(jnp.int32, (16, 128), 1)
    line = lax.broadcasted_iota(jnp.int32, (16, 128), 0)
    free_q = jnp.broadcast_to(free_ref[pl.ds(x, 1), :].astype(F32), (16, 128))
    free_q = jnp.sum(jnp.where(lane == (z * 4 + y) * 16 + line, free_q, 0.0), axis=1, keepdims=True)
    nu_v[...] = free_q + free_ref[pl.ds(row, 1), :].astype(F32)

    pl.semaphore_wait(barrier, 16 + gq_far.astype(jnp.int32))

    def s1(t, g, dz, db):
        beta = (axis_b(t) + db + g) % 4
        at = t * 32 + g * 8 + dz * 4 + db
        return pltpu.make_async_remote_copy(
            src_ref=gl.at[t, beta],
            dst_ref=ag.at[t, beta, :, x, z, y],
            send_sem=s1_send.at[at],
            recv_sem=s1_recv.at[at],
            device_id=(row, moved(t, 0, dz, db)),
            device_id_type=MESH,
        )

    def gq_copy(t, g):
        second = (1 - t) * ((x % 2) * 2 + z) + t * row
        beta = (second + g) % 4
        return pltpu.make_async_remote_copy(
            src_ref=gl.at[t, beta],
            dst_ref=gqb.at[t, beta, :, y],
            send_sem=gq_send.at[t * 16 + g * 4],
            recv_sem=gq_recv.at[t * 16 + g * 4],
            device_id=gq_target,
            device_id_type=MESH,
        )

    def gq_arrival(t, g):
        beta = (axis_b(t) + g) % 4
        return pltpu.make_async_remote_copy(
            src_ref=gl.at[t, beta],
            dst_ref=gqb.at[t, beta, :, row],
            send_sem=gq_send.at[t * 16 + g * 4],
            recv_sem=gq_recv.at[t * 16 + g * 4],
            device_id=gq_target,
            device_id_type=MESH,
        )

    def gq_row_copy(t, g, dr):
        beta = (axis_b(t) + g) % 4
        block = gqb.at[t, beta, :, row]
        return pltpu.make_async_remote_copy(
            src_ref=block,
            dst_ref=block,
            send_sem=gq_send.at[t * 16 + g * 4 + dr],
            recv_sem=gq_recv.at[t * 16 + g * 4 + dr],
            device_id=((row + dr) % 4, col),
            device_id_type=MESH,
        )

    def gq_row_arrival(t, g, dr):
        beta = (axis_b(t) + g) % 4
        return pltpu.make_async_remote_copy(
            src_ref=gl.at[t, beta],
            dst_ref=gqb.at[t, beta, :, (row + 4 - dr) % 4],
            send_sem=gq_send.at[t * 16 + g * 4 + dr],
            recv_sem=gq_recv.at[t * 16 + g * 4 + dr],
            device_id=((row + dr) % 4, col),
            device_id_type=MESH,
        )

    def s3(t, g, s):
        at = t * 16 + g * 4 + s
        beta = (axis_b(t) + g) % 4
        block = ag.at[0, beta, :, x] if t == 0 else ag.at[1, beta, :, :, :, y]
        return pltpu.make_async_remote_copy(
            src_ref=block,
            dst_ref=block,
            send_sem=s3_send.at[at],
            recv_sem=s3_recv.at[at],
            device_id=(row, moved(t, s, 0, 0)),
            device_id_type=MESH,
        )

    plane = [(dz, db) for dz in range(2) for db in range(4) if (dz, db) != (0, 0)]

    def start_s1(g):
        for dz, db in plane:
            for t in range(2):
                s1(t, g, dz, db).start()

    def start_gq(g):
        @pl.when(gq_far)
        def _():
            for t in range(2):
                gq_copy(t, g).start()

    def forward_gq(g):
        @pl.when(gq_from_far)
        def _():
            for t in range(2):
                gq_arrival(t, g).wait_recv()

        for t in range(2):
            for dr in (1, 2, 3):
                gq_row_copy(t, g, dr).start()

    def start_s3(g):
        for t in range(2):
            for dz, db in plane:
                s1(t, g, dz, db).wait_recv()
            for s in (1, 2, 3):
                s3(t, g, s).start()

    start_s1(1)
    start_gq(1)
    for g in (2, 3, 0):
        start_s1(g)
        start_gq(g)
    start_s3(1)
    forward_gq(1)
    vis_copy.wait()
    flag_copy.wait()

    def send1(n):
        t, g, s, _, _ = step(n)
        at = t * 16 + g * 4 + s
        return pltpu.make_async_remote_copy(
            src_ref=slabs.at[n],
            dst_ref=r1.at[t, g, s - 1],
            send_sem=p1_send.at[at],
            recv_sem=p1_recv.at[at],
            device_id=(row, moved(t, s, 0, 0)),
            device_id_type=MESH,
        )

    def send2(t, g):
        at = t * 4 + g
        return pltpu.make_async_remote_copy(
            src_ref=p1.at[t, g],
            dst_ref=r2.at[t, g - 1],
            send_sem=p2_send.at[at],
            recv_sem=p2_recv.at[at],
            device_id=(row, moved(t, 0, 0, g)),
            device_id_type=MESH,
        )

    send3 = pltpu.make_async_remote_copy(
        src_ref=p2.at[1 - z],
        dst_ref=r3,
        send_sem=p3_send,
        recv_sem=p3_recv,
        device_id=(row, moved(0, 0, 1, 0)),
        device_id_type=MESH,
    )

    def sum1(t, gi):
        g = (gi + 1) % 4
        for i in range(3):
            send1(gi * 8 + 2 * i + t).wait_recv()
        p1[t, g] = slabs[gi * 8 + 6 + t] + r1[t, g, 0] + r1[t, g, 1] + r1[t, g, 2]

    def body(n, carry):
        t, g, s, alpha, beta = step(n)
        load(n).wait()

        for tt in range(2):
            @pl.when(jnp.logical_and(s == 1, t == tt))
            def _():
                for i in (1, 2, 3):
                    s3(tt, g, i).wait_recv()
                    gq_row_arrival(tt, g, i).wait_recv()

        @pl.when(jnp.logical_and(n % 2 == 1, n < 6))
        def _():
            start_s3((n // 2 + 2) % 4)
            forward_gq((n // 2 + 2) % 4)

        gains = ag[t, beta, alpha].reshape(128, 128).T
        prepare_gains(gains, gqb[t, beta, alpha].reshape(16, 128), gv, tab)

        @pl.when(n >= 30)
        def _():
            gsv[t] = gains

        c = channel_of(t, alpha, beta)
        channel_sums(
            coh_v.at[n], vis_v.at[c], flag_v[c], nu_v[...], gv, tab, ys, wr, red, slabs.at[n]
        )

        @pl.when(s != 0)
        def _():
            send1(n).start()

        @pl.when(jnp.logical_and(s == 2, n >= 8))
        def _():
            sum1(t, n // 8 - 1)
            send2(t, n // 8).start()

        return carry

    lax.fori_loop(0, 32, body, 0)

    for t in range(2):
        sum1(t, 3)
        for g in (1, 2, 3):
            send2(t, g).wait_recv()
        p2[t] = p1[t, 0] + r2[t, 0] + r2[t, 1] + r2[t, 2]
    send3.start()
    send3.wait_recv()
    fresh = updated(gsv[z], p2[z] + r3[...]).T
    for d in range(32):
        fsrc[d] = fresh[d * 4 : d * 4 + 4]

    def f1_copy(dx):
        return pltpu.make_async_remote_copy(
            src_ref=fsrc.at[pl.ds(((x + dx) % 4) * 8, 8)],
            dst_ref=f1.at[x],
            send_sem=f1_send.at[dx],
            recv_sem=f1_recv.at[dx],
            device_id=(row, moved(0, dx, 0, 0)),
            device_id_type=MESH,
        )

    def f2_copy(dz, dy):
        zz = (z + dz) % 2
        yy = (y + dy) % 4
        return pltpu.make_async_remote_copy(
            src_ref=f1.at[:, zz * 4 + yy],
            dst_ref=fin.at[:, z * 4 + y],
            send_sem=f2_send.at[dz * 4 + dy],
            recv_sem=f2_recv.at[dz * 4 + dy],
            device_id=(row, moved(0, 0, dz, dy)),
            device_id_type=MESH,
        )

    for dx in (1, 2, 3):
        f1_copy(dx).start()
    f1[x] = fsrc[pl.ds(x * 8, 8)]
    for dx in (1, 2, 3):
        f1_copy(dx).wait_recv()
    for dz, dy in plane:
        f2_copy(dz, dy).start()
    fin[:, z * 4 + y] = f1[:, z * 4 + y]
    for dz, dy in plane:
        f2_copy(dz, dy).wait_recv()

    def drain_gains(g, carry):
        for t in range(2):
            for dz, db in plane:
                s1(t, g, dz, db).wait_send()
            for s in (1, 2, 3):
                s3(t, g, s).wait_send()
            for dr in (1, 2, 3):
                gq_row_copy(t, g, dr).wait_send()

            @pl.when(gq_far)
            def _():
                gq_copy(t, g).wait_send()

        return carry

    lax.fori_loop(0, 4, drain_gains, 0)

    def drain(n, carry):
        @pl.when((n // 2 + 1) % 4 != 0)
        def _():
            send1(n).wait_send()
        return carry

    lax.fori_loop(0, 32, drain, 0)
    for t in range(2):
        for g in (1, 2, 3):
            send2(t, g).wait_send()
    send3.wait_send()
    for dx in (1, 2, 3):
        f1_copy(dx).wait_send()
    for dz, dy in plane:
        f2_copy(dz, dy).wait_send()


def per_device(visibilities, coherencies, flags, freedom, gains):
    own = jnp.transpose(gains, (1, 2, 3, 0)).reshape(128, 4, 32)
    vmem = pl.BlockSpec(memory_space=pltpu.VMEM)
    hbm = pl.BlockSpec(memory_space=pl.ANY)
    dma = pltpu.SemaphoreType.DMA
    slab = (192, 128)
    fin = pl.pallas_call(
        kernel,
        out_shape=jax.ShapeDtypeStruct((4, 8, 4, 128), F32),
        in_specs=[hbm, hbm, hbm, vmem, vmem],
        out_specs=vmem,
        scratch_shapes=[
            pltpu.VMEM((32, 16, 8, 16, 128), BF16),
            pltpu.VMEM((32, 8, 16, 128), BF16),
            pltpu.VMEM((32, 16, 128), jnp.int32),
            pltpu.VMEM((2, 4, 4, 4, 2, 4, 4, 128), F32),
            pltpu.VMEM((2, 4, 4, 4, 4, 128), F32),
            pltpu.VMEM((3, 64, 128), F32),
            pltpu.VMEM((6, 16, 128), F32),
            pltpu.VMEM((16, 12, 16, 128), F32),
            pltpu.VMEM((13, 16, 128), F32),
            pltpu.VMEM((1536, 128), F32),
            pltpu.VMEM((16, 128), F32),
            pltpu.VMEM((2, 128, 128), F32),
            pltpu.VMEM((32,) + slab, F32),
            pltpu.VMEM((2, 4, 3) + slab, F32),
            pltpu.VMEM((2, 4) + slab, F32),
            pltpu.VMEM((2, 3) + slab, F32),
            pltpu.VMEM((2,) + slab, F32),
            pltpu.VMEM(slab, F32),
            pltpu.VMEM((32, 4, 128), F32),
            pltpu.VMEM((4, 8, 4, 128), F32),
            pltpu.VMEM((2, 4, 4, 4, 128), F32),
            dma((34,)),
            dma((64,)), dma((64,)),
            dma((32,)), dma((32,)),
            dma((32,)), dma((32,)),
            dma((32,)), dma((32,)),
            dma((8,)), dma((8,)),
            dma, dma,
            dma((4,)), dma((4,)),
            dma((8,)), dma((8,)),
        ],
        compiler_params=pltpu.CompilerParams(
            collective_id=0, has_side_effects=True, vmem_limit_bytes=56 * 2**20
        ),
        cost_estimate=pl.CostEstimate(flops=10**9, bytes_accessed=2 * 10**7, transcendentals=0),
    )(
        visibilities.reshape(32, 8, 16, 128),
        coherencies.reshape(32, 16, 8, 16, 128),
        flags.reshape(32, 16, 128),
        freedom.reshape(4, 128),
        own,
    )
    return jnp.transpose(fin.reshape(32, 4, 8, 16), (0, 2, 3, 1))


def solution(mesh):
    return jax.shard_map(
        per_device,
        mesh=mesh,
        in_specs=(
            P(None, None, None, "col", "row"),
            P(None, None, None, None, "col", "row"),
            P(None, None, "col", "row"),
            P(),
            P(None, None, None, ("row", "col")),
        ),
        out_specs=P(None, None, None, ("row", "col")),
        check_vma=False,
    )
```

```python
import jax
import jax.numpy as jnp
from jax import lax
from jax.experimental import pallas as pl
from jax.experimental.pallas import tpu as pltpu
from jax.sharding import PartitionSpec as P

F32 = jnp.float32
BF16 = jnp.bfloat16
MESH = pl.DeviceIdType.MESH
damping = 1.0


def product(a, b):
    out = [None] * 8
    for i in range(2):
        for j in range(2):
            real = (
                a[2 * i] * b[j]
                - a[4 + 2 * i] * b[4 + j]
                + a[2 * i + 1] * b[2 + j]
                - a[5 + 2 * i] * b[6 + j]
            )
            imag = (
                a[2 * i] * b[4 + j]
                + a[4 + 2 * i] * b[j]
                + a[2 * i + 1] * b[6 + j]
                + a[5 + 2 * i] * b[2 + j]
            )
            out[2 * i + j] = real
            out[4 + 2 * i + j] = imag
    return out


def prepare_gains(g, gq, gv, tab):
    a = g[:64]
    b = g[64:]
    gv[0] = a
    gv[1] = a + b
    gv[2] = b - a
    r = jnp.concatenate([gq] * 8, axis=0).T
    lane = lax.broadcasted_iota(jnp.int32, (16, 128), 1)
    sec = (lane // 16) % 4
    low = lane >= 64

    def pick(u0, u1, u2, u3):
        return jnp.where(sec == 0, u0, jnp.where(sec == 1, u1, jnp.where(sec == 2, u2, u3)))

    for j in range(2):
        r0, r1, i0, i1 = (r[m * 16 : m * 16 + 16] for m in (2 * j, 2 * j + 1, 4 + 2 * j, 5 + 2 * j))
        rows = [pick(r0, r1, i0, i1), pick(-i0, -i1, r0, r1), pick(r0 - i0, r1 - i1, i0 + r0, i1 + r1)]
        for v in range(3):
            hi = rows[v].astype(BF16).astype(F32)
            tab[j * 3 + v] = jnp.where(low, rows[v] - hi, hi)


def channel_sums(coh, vis, flag, nu, gv, tab, ys, wr, red, slab):
    lane = lax.broadcasted_iota(jnp.int32, (16, 128), 1)
    line = lax.broadcasted_iota(jnp.int32, (16, 128), 0)
    diag = (lane % 16) == line
    acc = [[jnp.zeros((16, 128), F32) for _ in range(3)] for _ in range(4)]
    for k in range(16):
        lhs = jnp.concatenate([jnp.where(diag, tab[g, k : k + 1, :], 0.0) for g in range(6)], axis=0).astype(BF16)
        half = jnp.concatenate(
            [
                jnp.concatenate([coh[k, 4 * ri + l], coh[k, 4 * ri + 2 + l]], axis=1)
                for ri in range(2)
                for l in range(2)
            ],
            axis=0,
        )
        out = jnp.dot(lhs, jnp.concatenate([half, half], axis=0), preferred_element_type=F32)
        y = {}
        for i in range(2):
            for j in range(2):
                for v in range(3):
                    t = out[(j * 3 + v) * 16 : (j * 3 + v) * 16 + 16, i * 128 : i * 128 + 128]
                    y[i, j, v] = t
                    ys[k, (i * 2 + j) * 3 + v] = t
        for i in range(2):
            for j in range(2):
                for l in range(2):
                    at = (2 * i + l) * 16 + k
                    ga, gs, gd = (gv[v, at : at + 1, :] for v in range(3))
                    part = acc[2 * i + j]
                    part[0] = part[0] + ga * y[l, j, 2]
                    part[1] = part[1] + gs * y[l, j, 1]
                    part[2] = part[2] + gd * y[l, j, 0]
    resid = []
    energy = None
    for m in range(4):
        re = vis[m].astype(F32) - (acc[m][0] - acc[m][1])
        im = vis[4 + m].astype(F32) - (acc[m][0] + acc[m][2])
        resid.append((re, im))
        t = re * re + im * im
        energy = t if energy is None else energy + t
    w = flag.astype(F32) * (nu + 8.0) / (nu + energy)
    for m in range(4):
        a = w * resid[m][0]
        b = w * resid[m][1]
        wr[m * 3] = a
        wr[m * 3 + 1] = a - b
        wr[m * 3 + 2] = a + b
    wr[12] = w
    for k in range(16):
        tot = [None] * 12
        cross = [[None] * 3 for _ in range(4)]
        for h in range(2):
            s = slice(8 * h, 8 * h + 8)
            y = [[[ys[k, (i * 2 + j) * 3 + v, s] for v in range(3)] for j in range(2)] for i in range(2)]
            for i in range(2):
                for j in range(2):
                    for l in range(2):
                        yr, yi, both = y[j][l]
                        at = (2 * i + l) * 3
                        terms = (wr[at, s] * both, wr[at + 1, s] * yi, wr[at + 2, s] * yr)
                        part = cross[2 * i + j]
                        for v in range(3):
                            part[v] = terms[v] if part[v] is None else part[v] + terms[v]
            (r00, i00, _), (r01, i01, _) = y[0]
            (r10, i10, _), (r11, i11, _) = y[1]
            every = (
                r00 * r00 + i00 * i00 + r01 * r01 + i01 * i01,
                r10 * r10 + i10 * i10 + r11 * r11 + i11 * i11,
                r00 * r10 + i00 * i10 + r01 * r11 + i01 * i11,
                i00 * r10 - r00 * i10 + i01 * r11 - r01 * i11,
            )
            for t in range(4):
                x = wr[12, s] * every[t]
                tot[8 + t] = x if h == 0 else tot[8 + t] + x
        for m in range(4):
            tot[m] = cross[m][0] - cross[m][1]
            tot[4 + m] = cross[m][2] - cross[m][0]
        for t in range(12):
            red[pl.ds((t * 16 + k) * 8, 8), :] = tot[t]
    for b in range(24):
        s = None
        for j in range(8):
            x = red[pl.ds(b * 64 + j, 8, stride=8), :]
            s = x if s is None else s + x
        slab[pl.ds(b * 8, 8), :] = s


def updated(g, total):
    share = [total[t * 16 : t * 16 + 16] for t in range(12)]
    upper_a = share[8] + damping
    lower_d = share[9] + damping
    part_re = share[10]
    part_im = share[11]
    determ = upper_a * lower_d - part_re * part_re - part_im * part_im
    zeros = jnp.zeros_like(upper_a)
    inverse = [
        lower_d / determ,
        -part_re / determ,
        -part_re / determ,
        upper_a / determ,
        zeros,
        -part_im / determ,
        part_im / determ,
        zeros,
    ]
    return g + jnp.concatenate(product(share[:8], inverse), axis=0)


def kernel(
    vis_hbm, coh_hbm, flag_hbm, free_ref, own_ref, fin,
    coh_v, vis_v, flag_v, ag, gqb, gv, tab, ys, wr, red, nu_v, gsv,
    slabs, r1, p1, r2, p2, r3, fsrc, f1,
    gl, load_sem, s1_send, s1_recv, gq_send, gq_recv, s3_send, s3_recv,
    p1_send, p1_recv, p2_send, p2_recv, p3_send, p3_recv, f1_send, f1_recv, f2_send, f2_recv,
):
    row = lax.axis_index("row")
    col = lax.axis_index("col")
    x = col // 8
    z = (col // 4) % 2
    y = col % 4

    def col_of(xx, zz, yy):
        return xx * 8 + zz * 4 + yy

    def moved(t, da, dz, db):
        return col_of((x + (1 - t) * da + t * db) % 4, (z + dz) % 2, (y + t * da + (1 - t) * db) % 4)

    def axis_a(t):
        return x + t * (y - x)

    def axis_b(t):
        return y + t * (x - y)

    def relay_side(t, g):
        return 1 + 2 * ((t + g) % 2)

    lead = 4

    def flag_of(cond):
        return cond.astype(jnp.int32)

    def step(n):
        m = n - lead
        first = flag_of(n < lead)
        last = flag_of(n >= 32 - lead)
        between = (1 - first) * (1 - last)
        mine = last + between * (1 - m % 2)
        j = first * n + last * (n - 16) + between * (m // 2 + (m % 2) * lead)
        t = mine * z + (1 - mine) * (1 - z)
        g = (j // 4 + 1) % 4
        i = j % 4
        d = relay_side(t, g)
        s = 2 * flag_of(i == 0) + (4 - d) * flag_of(i == 1) + d * flag_of(i == 2)
        alpha = (axis_a(t) + s) % 4
        beta = (axis_b(t) + g) % 4
        return t, j, g, s, alpha, beta

    def channel_of(t, alpha, beta):
        return (1 - t) * (alpha * 8 + beta) + t * (beta * 8 + 4 + alpha)

    def load(n):
        t, _, _, _, alpha, beta = step(n)
        return pltpu.make_async_copy(coh_hbm.at[channel_of(t, alpha, beta)], coh_v.at[n], load_sem.at[n])

    vis_copy = pltpu.make_async_copy(vis_hbm, vis_v, load_sem.at[32])
    flag_copy = pltpu.make_async_copy(flag_hbm, flag_v, load_sem.at[33])

    gq_target = (y, col_of(row, x // 2, (x % 2) * 2 + z))
    gq_source = (x, col_of(z * 2 + y // 2, y % 2, row))
    gq_far = jnp.logical_or(gq_target[0] != row, gq_target[1] != col)
    gq_from_far = jnp.logical_or(gq_source[0] != row, gq_source[1] != col)

    peers = [moved(0, da, 0, 0) for da in (1, 2, 3)]
    peers += [moved(0, 0, dz, db) for dz in range(2) for db in range(4) if (dz, db) != (0, 0)]
    peers += [moved(0, da, 1, 0) for da in (1, 2, 3)]
    barrier = pltpu.get_barrier_semaphore()
    for peer in peers:
        pl.semaphore_signal(barrier, inc=1, device_id=(row, peer), device_id_type=MESH)
    for dr in (1, 2, 3):
        pl.semaphore_signal(barrier, inc=1, device_id=((row + dr) % 4, col), device_id_type=MESH)

    @pl.when(gq_from_far)
    def _():
        pl.semaphore_signal(barrier, inc=1, device_id=gq_source, device_id_type=MESH)

    lax.fori_loop(0, 2, lambda n, u: (load(n).start(), u)[1], 0)
    vis_copy.start()
    flag_copy.start()
    lax.fori_loop(2, 32, lambda n, u: (load(n).start(), u)[1], 0)

    turned = jnp.concatenate([own_ref[:, p, :] for p in range(4)], axis=1).T
    for p in range(4):
        for cx in range(4):
            for cy in range(4):
                for t, beta, alpha in ((0, cy, cx), (1, cx, cy)):
                    at = p * 32 + cx * 8 + t * 4 + cy
                    gl[t, beta, alpha, p : p + 1] = turned[at : at + 1]
    for t in range(2):
        ag[t, :, :, x, z, y] = gl[t]

    @pl.when(jnp.logical_not(gq_from_far))
    def _():
        for t in range(2):
            gqb[t, :, :, row] = gl[t]

    lane = lax.broadcasted_iota(jnp.int32, (16, 128), 1)
    line = lax.broadcasted_iota(jnp.int32, (16, 128), 0)
    free_q = jnp.broadcast_to(free_ref[pl.ds(x, 1), :].astype(F32), (16, 128))
    free_q = jnp.sum(jnp.where(lane == (z * 4 + y) * 16 + line, free_q, 0.0), axis=1, keepdims=True)
    nu_v[...] = free_q + free_ref[pl.ds(row, 1), :].astype(F32)

    pl.semaphore_wait(barrier, 16 + gq_far.astype(jnp.int32))

    def s1(t, g, dz, db):
        beta = (axis_b(t) + db + g) % 4
        at = t * 32 + g * 8 + dz * 4 + db
        return pltpu.make_async_remote_copy(
            src_ref=gl.at[t, beta],
            dst_ref=ag.at[t, beta, :, x, z, y],
            send_sem=s1_send.at[at],
            recv_sem=s1_recv.at[at],
            device_id=(row, moved(t, 0, dz, db)),
            device_id_type=MESH,
        )

    def gq_copy(t, g):
        second = (1 - t) * ((x % 2) * 2 + z) + t * row
        beta = (second + g) % 4
        return pltpu.make_async_remote_copy(
            src_ref=gl.at[t, beta],
            dst_ref=gqb.at[t, beta, :, y],
            send_sem=gq_send.at[t * 16 + g * 4],
            recv_sem=gq_recv.at[t * 16 + g * 4],
            device_id=gq_target,
            device_id_type=MESH,
        )

    def gq_arrival(t, g):
        beta = (axis_b(t) + g) % 4
        return pltpu.make_async_remote_copy(
            src_ref=gl.at[t, beta],
            dst_ref=gqb.at[t, beta, :, row],
            send_sem=gq_send.at[t * 16 + g * 4],
            recv_sem=gq_recv.at[t * 16 + g * 4],
            device_id=gq_target,
            device_id_type=MESH,
        )

    def gq_row_copy(t, g, dr):
        beta = (axis_b(t) + g) % 4
        block = gqb.at[t, beta, :, row]
        return pltpu.make_async_remote_copy(
            src_ref=block,
            dst_ref=block,
            send_sem=gq_send.at[t * 16 + g * 4 + dr],
            recv_sem=gq_recv.at[t * 16 + g * 4 + dr],
            device_id=((row + dr) % 4, col),
            device_id_type=MESH,
        )

    def gq_row_arrival(t, g, dr):
        beta = (axis_b(t) + g) % 4
        return pltpu.make_async_remote_copy(
            src_ref=gl.at[t, beta],
            dst_ref=gqb.at[t, beta, :, (row + 4 - dr) % 4],
            send_sem=gq_send.at[t * 16 + g * 4 + dr],
            recv_sem=gq_recv.at[t * 16 + g * 4 + dr],
            device_id=((row + dr) % 4, col),
            device_id_type=MESH,
        )

    def s3(t, g, s):
        at = t * 16 + g * 4 + s
        beta = (axis_b(t) + g) % 4
        block = ag.at[0, beta, :, x] if t == 0 else ag.at[1, beta, :, :, :, y]
        return pltpu.make_async_remote_copy(
            src_ref=block,
            dst_ref=block,
            send_sem=s3_send.at[at],
            recv_sem=s3_recv.at[at],
            device_id=(row, moved(t, s, 0, 0)),
            device_id_type=MESH,
        )

    plane = [(dz, db) for dz in range(2) for db in range(4) if (dz, db) != (0, 0)]

    def by_type(t, act):
        for tt in range(2):
            @pl.when(t == tt)
            def _():
                act(tt)

    def start_own(t, g):
        for dz, db in plane:
            s1(t, g, dz, db).start()

        @pl.when(gq_far)
        def _():
            gq_copy(t, g).start()

    def forward(t, g):
        for dz, db in plane:
            s1(t, g, dz, db).wait_recv()
        for s in (1, 2, 3):
            s3(t, g, s).start()

        @pl.when(gq_from_far)
        def _():
            gq_arrival(t, g).wait_recv()

        for dr in (1, 2, 3):
            gq_row_copy(t, g, dr).start()

    kept = z
    given = 1 - z
    start_own(0, 1)
    start_own(1, 1)
    start_own(0, 2)
    start_own(1, 2)
    by_type(given, lambda t: forward(t, 1))
    by_type(kept, lambda t: forward(t, 1))
    vis_copy.wait()
    flag_copy.wait()

    def send1(t, g, s, j):
        at = t * 16 + g * 4 + s
        return pltpu.make_async_remote_copy(
            src_ref=slabs.at[t * 16 + j],
            dst_ref=r1.at[t, g, s - 1],
            send_sem=p1_send.at[at],
            recv_sem=p1_recv.at[at],
            device_id=(row, moved(t, s, 0, 0)),
            device_id_type=MESH,
        )

    def relay(t, g, j):
        at = t * 16 + g * 4
        return pltpu.make_async_remote_copy(
            src_ref=slabs.at[t * 16 + j],
            dst_ref=r1.at[t, g, 1],
            send_sem=p1_send.at[at],
            recv_sem=p1_recv.at[at],
            device_id=(row, moved(t, relay_side(t, g), 0, 0)),
            device_id_type=MESH,
        )

    def send2(t, g):
        at = t * 4 + g
        return pltpu.make_async_remote_copy(
            src_ref=p1.at[t, g],
            dst_ref=r2.at[t, g - 1],
            send_sem=p2_send.at[at],
            recv_sem=p2_recv.at[at],
            device_id=(row, moved(t, 0, 0, g)),
            device_id_type=MESH,
        )

    send3 = pltpu.make_async_remote_copy(
        src_ref=p2.at[1 - z],
        dst_ref=r3,
        send_sem=p3_send,
        recv_sem=p3_recv,
        device_id=(row, moved(0, 0, 1, 0)),
        device_id_type=MESH,
    )

    def sum1(t, g, j):
        for i in (1, 3):
            send1(t, g, i, 0).wait_recv()
        p1[t, g] = slabs[t * 16 + j] + r1[t, g, 0] + r1[t, g, 2]

        @pl.when(g % 3 == 0)
        def _():
            send1(t, g, 2, 0).wait_recv()
            p1[t, g] = p1[t, g] + r1[t, g, 1]

    def sum2(t):
        sum1(t, 0, 15)
        for g in (1, 2, 3):
            send2(t, g).wait_recv()
        p2[t] = p1[t, 0] + r2[t, 0] + r2[t, 1] + r2[t, 2]

    def body(n, carry):
        t, j, g, s, alpha, beta = step(n)
        i = j % 4
        load(n).wait()

        def at(*steps):
            hit = n == steps[0]
            for other in steps[1:]:
                hit = jnp.logical_or(hit, n == other)
            return pl.when(hit)

        @at(0, 6, 14)
        def _():
            by_type(given, lambda tt: forward(tt, (2 + flag_of(n >= 6) + flag_of(n >= 14)) % 4))

        @at(5, 13, 21)
        def _():
            by_type(kept, lambda tt: forward(tt, (2 + flag_of(n >= 13) + flag_of(n >= 21)) % 4))

        @at(1, 8)
        def _():
            for tt in range(2):
                start_own(tt, (3 + flag_of(n >= 8)) % 4)

        for tt in range(2):
            @pl.when(jnp.logical_and(i == 0, t == tt))
            def _():
                for k in (1, 2, 3):
                    s3(tt, g, k).wait_recv()
                    gq_row_arrival(tt, g, k).wait_recv()

        gains = ag[t, beta, alpha].reshape(128, 128).T
        prepare_gains(gains, gqb[t, beta, alpha].reshape(16, 128), gv, tab)

        @pl.when(j == 15)
        def _():
            gsv[t] = gains

        c = channel_of(t, alpha, beta)
        channel_sums(
            coh_v.at[n], vis_v.at[c], flag_v[c], nu_v[...], gv, tab, ys, wr, red, slabs.at[t * 16 + j]
        )

        direct = g % 3 == 0

        @pl.when(jnp.logical_or(i == 1, jnp.logical_and(direct, i != 3)))
        def _():
            send1(t, g, s, j).start()

        @pl.when(jnp.logical_and(jnp.logical_not(direct), i == 0))
        def _():
            relay(t, g, j).start()

        @pl.when(jnp.logical_and(jnp.logical_not(direct), i == 3))
        def _():
            relay(t, g, j).wait_recv()
            slabs[t * 16 + j - 1] = slabs[t * 16 + j - 1] + r1[t, g, 1]
            send1(t, g, relay_side(t, g), j - 1).start()

        @pl.when(jnp.logical_or(j == 6, jnp.logical_or(j == 10, j == 13)))
        def _():
            sum1(t, j // 4, (j // 4) * 4 - 1)
            send2(t, j // 4).start()

        @pl.when(n == 29)
        def _():
            sum2(given)
            send3.start()

        return carry

    lax.fori_loop(0, 32, body, 0)

    sum2(kept)
    send3.wait_recv()
    fresh = updated(gsv[z], p2[z] + r3[...]).T
    for d in range(32):
        fsrc[d] = fresh[d * 4 : d * 4 + 4]

    def f1_copy(dx):
        return pltpu.make_async_remote_copy(
            src_ref=fsrc.at[pl.ds(((x + dx) % 4) * 8, 8)],
            dst_ref=f1.at[x],
            send_sem=f1_send.at[dx],
            recv_sem=f1_recv.at[dx],
            device_id=(row, moved(0, dx, 0, 0)),
            device_id_type=MESH,
        )

    def f2_copy(dz, dy):
        zz = (z + dz) % 2
        yy = (y + dy) % 4
        return pltpu.make_async_remote_copy(
            src_ref=f1.at[:, zz * 4 + yy],
            dst_ref=fin.at[:, z * 4 + y],
            send_sem=f2_send.at[dz * 4 + dy],
            recv_sem=f2_recv.at[dz * 4 + dy],
            device_id=(row, moved(0, 0, dz, dy)),
            device_id_type=MESH,
        )

    for dx in (1, 2, 3):
        f1_copy(dx).start()
    f1[x] = fsrc[pl.ds(x * 8, 8)]
    for dx in (1, 2, 3):
        f1_copy(dx).wait_recv()
    for dz, dy in plane:
        f2_copy(dz, dy).start()
    fin[:, z * 4 + y] = f1[:, z * 4 + y]
    for dz, dy in plane:
        f2_copy(dz, dy).wait_recv()

    def drain_gains(g, carry):
        for t in range(2):
            for dz, db in plane:
                s1(t, g, dz, db).wait_send()
            for s in (1, 2, 3):
                s3(t, g, s).wait_send()
            for dr in (1, 2, 3):
                gq_row_copy(t, g, dr).wait_send()

            @pl.when(gq_far)
            def _():
                gq_copy(t, g).wait_send()

        return carry

    lax.fori_loop(0, 4, drain_gains, 0)

    def drain(g, carry):
        for t in range(2):
            send1(t, g, 1, 0).wait_send()
            send1(t, g, 3, 0).wait_send()

            @pl.when(g % 3 == 0)
            def _():
                send1(t, g, 2, 0).wait_send()

            @pl.when(g % 3 != 0)
            def _():
                relay(t, g, 0).wait_send()

        return carry

    lax.fori_loop(0, 4, drain, 0)
    for t in range(2):
        for g in (1, 2, 3):
            send2(t, g).wait_send()
    send3.wait_send()
    for dx in (1, 2, 3):
        f1_copy(dx).wait_send()
    for dz, dy in plane:
        f2_copy(dz, dy).wait_send()


def per_device(visibilities, coherencies, flags, freedom, gains):
    own = jnp.transpose(gains, (1, 2, 3, 0)).reshape(128, 4, 32)
    vmem = pl.BlockSpec(memory_space=pltpu.VMEM)
    hbm = pl.BlockSpec(memory_space=pl.ANY)
    dma = pltpu.SemaphoreType.DMA
    slab = (192, 128)
    fin = pl.pallas_call(
        kernel,
        out_shape=jax.ShapeDtypeStruct((4, 8, 4, 128), F32),
        in_specs=[hbm, hbm, hbm, vmem, vmem],
        out_specs=vmem,
        scratch_shapes=[
            pltpu.VMEM((32, 16, 8, 16, 128), BF16),
            pltpu.VMEM((32, 8, 16, 128), BF16),
            pltpu.VMEM((32, 16, 128), jnp.int32),
            pltpu.VMEM((2, 4, 4, 4, 2, 4, 4, 128), F32),
            pltpu.VMEM((2, 4, 4, 4, 4, 128), F32),
            pltpu.VMEM((3, 64, 128), F32),
            pltpu.VMEM((6, 16, 128), F32),
            pltpu.VMEM((16, 12, 16, 128), F32),
            pltpu.VMEM((13, 16, 128), F32),
            pltpu.VMEM((1536, 128), F32),
            pltpu.VMEM((16, 128), F32),
            pltpu.VMEM((2, 128, 128), F32),
            pltpu.VMEM((32,) + slab, F32),
            pltpu.VMEM((2, 4, 3) + slab, F32),
            pltpu.VMEM((2, 4) + slab, F32),
            pltpu.VMEM((2, 3) + slab, F32),
            pltpu.VMEM((2,) + slab, F32),
            pltpu.VMEM(slab, F32),
            pltpu.VMEM((32, 4, 128), F32),
            pltpu.VMEM((4, 8, 4, 128), F32),
            pltpu.VMEM((2, 4, 4, 4, 128), F32),
            dma((34,)),
            dma((64,)), dma((64,)),
            dma((32,)), dma((32,)),
            dma((32,)), dma((32,)),
            dma((32,)), dma((32,)),
            dma((8,)), dma((8,)),
            dma, dma,
            dma((4,)), dma((4,)),
            dma((8,)), dma((8,)),
        ],
        compiler_params=pltpu.CompilerParams(
            collective_id=0, has_side_effects=True, vmem_limit_bytes=56 * 2**20
        ),
        cost_estimate=pl.CostEstimate(flops=10**9, bytes_accessed=2 * 10**7, transcendentals=0),
    )(
        visibilities.reshape(32, 8, 16, 128),
        coherencies.reshape(32, 16, 8, 16, 128),
        flags.reshape(32, 16, 128),
        freedom.reshape(4, 128),
        own,
    )
    return jnp.transpose(fin.reshape(32, 4, 8, 16), (0, 2, 3, 1))


def solution(mesh):
    return jax.shard_map(
        per_device,
        mesh=mesh,
        in_specs=(
            P(None, None, None, "col", "row"),
            P(None, None, None, None, "col", "row"),
            P(None, None, "col", "row"),
            P(),
            P(None, None, None, ("row", "col")),
        ),
        out_specs=P(None, None, None, ("row", "col")),
        check_vma=False,
    )
```

```python
import jax
import jax.numpy as jnp
from jax import lax
from jax.experimental import pallas as pl
from jax.experimental.pallas import tpu as pltpu
from jax.sharding import PartitionSpec as P

F32 = jnp.float32
BF16 = jnp.bfloat16
MESH = pl.DeviceIdType.MESH
damping = 1.0


def product(a, b):
    out = [None] * 8
    for i in range(2):
        for j in range(2):
            real = (
                a[2 * i] * b[j]
                - a[4 + 2 * i] * b[4 + j]
                + a[2 * i + 1] * b[2 + j]
                - a[5 + 2 * i] * b[6 + j]
            )
            imag = (
                a[2 * i] * b[4 + j]
                + a[4 + 2 * i] * b[j]
                + a[2 * i + 1] * b[6 + j]
                + a[5 + 2 * i] * b[2 + j]
            )
            out[2 * i + j] = real
            out[4 + 2 * i + j] = imag
    return out


def prepare_gains(g, gq, gv, tab):
    a = g[:64]
    b = g[64:]
    gv[0] = a
    gv[1] = a + b
    gv[2] = b - a
    r = jnp.concatenate([gq] * 8, axis=0).T
    lane = lax.broadcasted_iota(jnp.int32, (16, 128), 1)
    sec = (lane // 16) % 4
    low = lane >= 64

    def pick(u0, u1, u2, u3):
        return jnp.where(sec == 0, u0, jnp.where(sec == 1, u1, jnp.where(sec == 2, u2, u3)))

    for j in range(2):
        r0, r1, i0, i1 = (r[m * 16 : m * 16 + 16] for m in (2 * j, 2 * j + 1, 4 + 2 * j, 5 + 2 * j))
        rows = [pick(r0, r1, i0, i1), pick(-i0, -i1, r0, r1), pick(r0 - i0, r1 - i1, i0 + r0, i1 + r1)]
        for v in range(3):
            hi = rows[v].astype(BF16).astype(F32)
            tab[j * 3 + v] = jnp.where(low, rows[v] - hi, hi)


def channel_sums(coh, vis, flag, nu, gv, tab, ys, wr, red, slab):
    lane = lax.broadcasted_iota(jnp.int32, (16, 128), 1)
    line = lax.broadcasted_iota(jnp.int32, (16, 128), 0)
    diag = (lane % 16) == line
    acc = [[jnp.zeros((16, 128), F32) for _ in range(3)] for _ in range(4)]
    for k in range(16):
        lhs = jnp.concatenate([jnp.where(diag, tab[g, k : k + 1, :], 0.0) for g in range(6)], axis=0).astype(BF16)
        half = jnp.concatenate(
            [
                jnp.concatenate([coh[k, 4 * ri + l], coh[k, 4 * ri + 2 + l]], axis=1)
                for ri in range(2)
                for l in range(2)
            ],
            axis=0,
        )
        out = jnp.dot(lhs, jnp.concatenate([half, half], axis=0), preferred_element_type=F32)
        y = {}
        for i in range(2):
            for j in range(2):
                for v in range(3):
                    t = out[(j * 3 + v) * 16 : (j * 3 + v) * 16 + 16, i * 128 : i * 128 + 128]
                    y[i, j, v] = t
                    ys[k, (i * 2 + j) * 3 + v] = t
        for i in range(2):
            for j in range(2):
                for l in range(2):
                    at = (2 * i + l) * 16 + k
                    ga, gs, gd = (gv[v, at : at + 1, :] for v in range(3))
                    part = acc[2 * i + j]
                    part[0] = part[0] + ga * y[l, j, 2]
                    part[1] = part[1] + gs * y[l, j, 1]
                    part[2] = part[2] + gd * y[l, j, 0]
    resid = []
    energy = None
    for m in range(4):
        re = vis[m].astype(F32) - (acc[m][0] - acc[m][1])
        im = vis[4 + m].astype(F32) - (acc[m][0] + acc[m][2])
        resid.append((re, im))
        t = re * re + im * im
        energy = t if energy is None else energy + t
    w = flag.astype(F32) * (nu + 8.0) / (nu + energy)
    for m in range(4):
        a = w * resid[m][0]
        b = w * resid[m][1]
        wr[m * 3] = a
        wr[m * 3 + 1] = a - b
        wr[m * 3 + 2] = a + b
    wr[12] = w
    for k in range(16):
        tot = [None] * 12
        cross = [[None] * 3 for _ in range(4)]
        for h in range(2):
            s = slice(8 * h, 8 * h + 8)
            y = [[[ys[k, (i * 2 + j) * 3 + v, s] for v in range(3)] for j in range(2)] for i in range(2)]
            for i in range(2):
                for j in range(2):
                    for l in range(2):
                        yr, yi, both = y[j][l]
                        at = (2 * i + l) * 3
                        terms = (wr[at, s] * both, wr[at + 1, s] * yi, wr[at + 2, s] * yr)
                        part = cross[2 * i + j]
                        for v in range(3):
                            part[v] = terms[v] if part[v] is None else part[v] + terms[v]
            (r00, i00, _), (r01, i01, _) = y[0]
            (r10, i10, _), (r11, i11, _) = y[1]
            every = (
                r00 * r00 + i00 * i00 + r01 * r01 + i01 * i01,
                r10 * r10 + i10 * i10 + r11 * r11 + i11 * i11,
                r00 * r10 + i00 * i10 + r01 * r11 + i01 * i11,
                i00 * r10 - r00 * i10 + i01 * r11 - r01 * i11,
            )
            for t in range(4):
                x = wr[12, s] * every[t]
                tot[8 + t] = x if h == 0 else tot[8 + t] + x
        for m in range(4):
            tot[m] = cross[m][0] - cross[m][1]
            tot[4 + m] = cross[m][2] - cross[m][0]
        for t in range(12):
            red[pl.ds((t * 16 + k) * 8, 8), :] = tot[t]
    for b in range(24):
        s = None
        for j in range(8):
            x = red[pl.ds(b * 64 + j, 8, stride=8), :]
            s = x if s is None else s + x
        slab[pl.ds(b * 8, 8), :] = s


def updated(g, total):
    share = [total[t * 16 : t * 16 + 16] for t in range(12)]
    upper_a = share[8] + damping
    lower_d = share[9] + damping
    part_re = share[10]
    part_im = share[11]
    determ = upper_a * lower_d - part_re * part_re - part_im * part_im
    zeros = jnp.zeros_like(upper_a)
    inverse = [
        lower_d / determ,
        -part_re / determ,
        -part_re / determ,
        upper_a / determ,
        zeros,
        -part_im / determ,
        part_im / determ,
        zeros,
    ]
    return g + jnp.concatenate(product(share[:8], inverse), axis=0)


def kernel(
    vis_hbm, coh_hbm, flag_hbm, free_ref, own_ref, fin,
    coh_v, vis_v, flag_v, ag, gqb, gv, tab, ys, wr, red, nu_v, gsv,
    slabs, r1, p1, r2, p2, r3, fsrc, f1,
    gl, load_sem, s1_send, s1_recv, gq_send, gq_recv, s3_send, s3_recv,
    p1_send, p1_recv, p2_send, p2_recv, p3_send, p3_recv, f1_send, f1_recv, f2_send, f2_recv,
):
    row = lax.axis_index("row")
    col = lax.axis_index("col")
    x = col // 8
    z = (col // 4) % 2
    y = col % 4

    def col_of(xx, zz, yy):
        return xx * 8 + zz * 4 + yy

    def moved(t, da, dz, db):
        return col_of((x + (1 - t) * da + t * db) % 4, (z + dz) % 2, (y + t * da + (1 - t) * db) % 4)

    def axis_a(t):
        return x + t * (y - x)

    def axis_b(t):
        return y + t * (x - y)

    def relay_side(t, g):
        return 1 + 2 * ((t + g) % 2)

    lead = 4

    def flag_of(cond):
        return cond.astype(jnp.int32)

    def step(n):
        m = n - lead
        first = flag_of(n < lead)
        last = flag_of(n >= 32 - lead)
        between = (1 - first) * (1 - last)
        mine = last + between * (1 - m % 2)
        j = first * n + last * (n - 16) + between * (m // 2 + (m % 2) * lead)
        t = mine * z + (1 - mine) * (1 - z)
        g = (j // 4 + 1) % 4
        i = j % 4
        d = relay_side(t, g)
        s = 2 * flag_of(i == 0) + (4 - d) * flag_of(i == 1) + d * flag_of(i == 2)
        alpha = (axis_a(t) + s) % 4
        beta = (axis_b(t) + g) % 4
        return t, j, g, s, alpha, beta

    def channel_of(t, alpha, beta):
        return (1 - t) * (alpha * 8 + beta) + t * (beta * 8 + 4 + alpha)

    def load(n):
        t, _, _, _, alpha, beta = step(n)
        return pltpu.make_async_copy(coh_hbm.at[channel_of(t, alpha, beta)], coh_v.at[n], load_sem.at[n])

    vis_copy = pltpu.make_async_copy(vis_hbm, vis_v, load_sem.at[32])
    flag_copy = pltpu.make_async_copy(flag_hbm, flag_v, load_sem.at[33])

    gq_target = (y, col_of(row, x // 2, (x % 2) * 2 + z))
    gq_source = (x, col_of(z * 2 + y // 2, y % 2, row))
    gq_far = jnp.logical_or(gq_target[0] != row, gq_target[1] != col)
    gq_from_far = jnp.logical_or(gq_source[0] != row, gq_source[1] != col)

    peers = [moved(0, da, 0, 0) for da in (1, 2, 3)]
    peers += [moved(0, 0, dz, db) for dz in range(2) for db in range(4) if (dz, db) != (0, 0)]
    peers += [moved(0, da, 1, 0) for da in (1, 2, 3)]
    barrier = pltpu.get_barrier_semaphore()
    for peer in peers:
        pl.semaphore_signal(barrier, inc=1, device_id=(row, peer), device_id_type=MESH)
    for dr in (1, 2, 3):
        pl.semaphore_signal(barrier, inc=1, device_id=((row + dr) % 4, col), device_id_type=MESH)

    @pl.when(gq_from_far)
    def _():
        pl.semaphore_signal(barrier, inc=1, device_id=gq_source, device_id_type=MESH)

    lax.fori_loop(0, 2, lambda n, u: (load(n).start(), u)[1], 0)
    vis_copy.start()
    flag_copy.start()
    lax.fori_loop(2, 32, lambda n, u: (load(n).start(), u)[1], 0)

    turned = jnp.concatenate([own_ref[:, p, :] for p in range(4)], axis=1).T
    for p in range(4):
        for cx in range(4):
            for cy in range(4):
                for t, beta, alpha in ((0, cy, cx), (1, cx, cy)):
                    at = p * 32 + cx * 8 + t * 4 + cy
                    gl[t, beta, alpha, p : p + 1] = turned[at : at + 1]
    for t in range(2):
        ag[t, :, :, x, z, y] = gl[t]

    @pl.when(jnp.logical_not(gq_from_far))
    def _():
        for t in range(2):
            gqb[t, :, :, row] = gl[t]

    lane = lax.broadcasted_iota(jnp.int32, (16, 128), 1)
    line = lax.broadcasted_iota(jnp.int32, (16, 128), 0)
    free_q = jnp.broadcast_to(free_ref[pl.ds(x, 1), :].astype(F32), (16, 128))
    free_q = jnp.sum(jnp.where(lane == (z * 4 + y) * 16 + line, free_q, 0.0), axis=1, keepdims=True)
    nu_v[...] = free_q + free_ref[pl.ds(row, 1), :].astype(F32)

    pl.semaphore_wait(barrier, 16 + gq_far.astype(jnp.int32))

    def s1(t, g, dz, db):
        beta = (axis_b(t) + db + g) % 4
        at = t * 32 + g * 8 + dz * 4 + db
        return pltpu.make_async_remote_copy(
            src_ref=gl.at[t, beta],
            dst_ref=ag.at[t, beta, :, x, z, y],
            send_sem=s1_send.at[at],
            recv_sem=s1_recv.at[at],
            device_id=(row, moved(t, 0, dz, db)),
            device_id_type=MESH,
        )

    def gq_copy(t, g):
        second = (1 - t) * ((x % 2) * 2 + z) + t * row
        beta = (second + g) % 4
        return pltpu.make_async_remote_copy(
            src_ref=gl.at[t, beta],
            dst_ref=gqb.at[t, beta, :, y],
            send_sem=gq_send.at[t * 16 + g * 4],
            recv_sem=gq_recv.at[t * 16 + g * 4],
            device_id=gq_target,
            device_id_type=MESH,
        )

    def gq_arrival(t, g):
        beta = (axis_b(t) + g) % 4
        return pltpu.make_async_remote_copy(
            src_ref=gl.at[t, beta],
            dst_ref=gqb.at[t, beta, :, row],
            send_sem=gq_send.at[t * 16 + g * 4],
            recv_sem=gq_recv.at[t * 16 + g * 4],
            device_id=gq_target,
            device_id_type=MESH,
        )

    def gq_row_copy(t, g, dr):
        beta = (axis_b(t) + g) % 4
        block = gqb.at[t, beta, :, row]
        return pltpu.make_async_remote_copy(
            src_ref=block,
            dst_ref=block,
            send_sem=gq_send.at[t * 16 + g * 4 + dr],
            recv_sem=gq_recv.at[t * 16 + g * 4 + dr],
            device_id=((row + dr) % 4, col),
            device_id_type=MESH,
        )

    def gq_row_arrival(t, g, dr):
        beta = (axis_b(t) + g) % 4
        return pltpu.make_async_remote_copy(
            src_ref=gl.at[t, beta],
            dst_ref=gqb.at[t, beta, :, (row + 4 - dr) % 4],
            send_sem=gq_send.at[t * 16 + g * 4 + dr],
            recv_sem=gq_recv.at[t * 16 + g * 4 + dr],
            device_id=((row + dr) % 4, col),
            device_id_type=MESH,
        )

    def s3(t, g, s):
        at = t * 16 + g * 4 + s
        beta = (axis_b(t) + g) % 4
        block = ag.at[0, beta, :, x] if t == 0 else ag.at[1, beta, :, :, :, y]
        return pltpu.make_async_remote_copy(
            src_ref=block,
            dst_ref=block,
            send_sem=s3_send.at[at],
            recv_sem=s3_recv.at[at],
            device_id=(row, moved(t, s, 0, 0)),
            device_id_type=MESH,
        )

    plane = [(dz, db) for dz in range(2) for db in range(4) if (dz, db) != (0, 0)]

    def by_type(t, act):
        for tt in range(2):
            @pl.when(t == tt)
            def _():
                act(tt)

    def start_own(t, g):
        for dz, db in plane:
            s1(t, g, dz, db).start()

        @pl.when(gq_far)
        def _():
            gq_copy(t, g).start()

    def forward(t, g):
        for dz, db in plane:
            s1(t, g, dz, db).wait_recv()
        for s in (1, 2, 3):
            s3(t, g, s).start()

        @pl.when(gq_from_far)
        def _():
            gq_arrival(t, g).wait_recv()

        for dr in (1, 2, 3):
            gq_row_copy(t, g, dr).start()

    kept = z
    given = 1 - z
    start_own(0, 1)
    start_own(1, 1)
    start_own(0, 2)
    start_own(1, 2)
    by_type(given, lambda t: forward(t, 1))
    by_type(kept, lambda t: forward(t, 1))
    vis_copy.wait()
    flag_copy.wait()

    def send1(t, g, s, j):
        at = t * 16 + g * 4 + s
        return pltpu.make_async_remote_copy(
            src_ref=slabs.at[t * 16 + j],
            dst_ref=r1.at[t, g, s - 1],
            send_sem=p1_send.at[at],
            recv_sem=p1_recv.at[at],
            device_id=(row, moved(t, s, 0, 0)),
            device_id_type=MESH,
        )

    def send2(t, g):
        at = t * 4 + g
        return pltpu.make_async_remote_copy(
            src_ref=p1.at[t, g],
            dst_ref=r2.at[t, g - 1],
            send_sem=p2_send.at[at],
            recv_sem=p2_recv.at[at],
            device_id=(row, moved(t, 0, 0, g)),
            device_id_type=MESH,
        )

    send3 = pltpu.make_async_remote_copy(
        src_ref=p2.at[1 - z],
        dst_ref=r3,
        send_sem=p3_send,
        recv_sem=p3_recv,
        device_id=(row, moved(0, 0, 1, 0)),
        device_id_type=MESH,
    )

    def sum1(t, g, j):
        for i in (1, 2, 3):
            send1(t, g, i, 0).wait_recv()
        p1[t, g] = slabs[t * 16 + j] + r1[t, g, 0] + r1[t, g, 1] + r1[t, g, 2]

    def sum2(t):
        sum1(t, 0, 15)
        for g in (1, 2, 3):
            send2(t, g).wait_recv()
        p2[t] = p1[t, 0] + r2[t, 0] + r2[t, 1] + r2[t, 2]

    def body(n, carry):
        t, j, g, s, alpha, beta = step(n)
        i = j % 4
        load(n).wait()

        def at(*steps):
            hit = n == steps[0]
            for other in steps[1:]:
                hit = jnp.logical_or(hit, n == other)
            return pl.when(hit)

        @at(0, 6, 14)
        def _():
            by_type(given, lambda tt: forward(tt, (2 + flag_of(n >= 6) + flag_of(n >= 14)) % 4))

        @at(5, 13, 21)
        def _():
            by_type(kept, lambda tt: forward(tt, (2 + flag_of(n >= 13) + flag_of(n >= 21)) % 4))

        @at(1, 8)
        def _():
            for tt in range(2):
                start_own(tt, (3 + flag_of(n >= 8)) % 4)

        for tt in range(2):
            @pl.when(jnp.logical_and(i == 0, t == tt))
            def _():
                for k in (1, 2, 3):
                    s3(tt, g, k).wait_recv()
                    gq_row_arrival(tt, g, k).wait_recv()

        gains = ag[t, beta, alpha].reshape(128, 128).T
        prepare_gains(gains, gqb[t, beta, alpha].reshape(16, 128), gv, tab)

        @pl.when(j == 15)
        def _():
            gsv[t] = gains

        c = channel_of(t, alpha, beta)
        channel_sums(
            coh_v.at[n], vis_v.at[c], flag_v[c], nu_v[...], gv, tab, ys, wr, red, slabs.at[t * 16 + j]
        )

        @pl.when(i != 3)
        def _():
            send1(t, g, s, j).start()

        @pl.when(jnp.logical_and(i == 1, j > 4))
        def _():
            sum1(t, j // 4, (j // 4) * 4 - 1)
            send2(t, j // 4).start()

        @pl.when(n == 29)
        def _():
            sum2(given)
            send3.start()

        return carry

    lax.fori_loop(0, 32, body, 0)

    def drain_gains(g, carry):
        for t in range(2):
            for dz, db in plane:
                s1(t, g, dz, db).wait_send()
            for s in (1, 2, 3):
                s3(t, g, s).wait_send()
            for dr in (1, 2, 3):
                gq_row_copy(t, g, dr).wait_send()

            @pl.when(gq_far)
            def _():
                gq_copy(t, g).wait_send()

        return carry

    lax.fori_loop(0, 4, drain_gains, 0)

    sum2(kept)
    send3.wait_recv()
    fresh = updated(gsv[z], p2[z] + r3[...]).T
    for d in range(32):
        fsrc[d] = fresh[d * 4 : d * 4 + 4]

    def f1_copy(dx):
        return pltpu.make_async_remote_copy(
            src_ref=fsrc.at[pl.ds(((x + dx) % 4) * 8, 8)],
            dst_ref=f1.at[x],
            send_sem=f1_send.at[dx],
            recv_sem=f1_recv.at[dx],
            device_id=(row, moved(0, dx, 0, 0)),
            device_id_type=MESH,
        )

    def f2_copy(dz, dy):
        zz = (z + dz) % 2
        yy = (y + dy) % 4
        return pltpu.make_async_remote_copy(
            src_ref=f1.at[:, zz * 4 + yy],
            dst_ref=fin.at[:, z * 4 + y],
            send_sem=f2_send.at[dz * 4 + dy],
            recv_sem=f2_recv.at[dz * 4 + dy],
            device_id=(row, moved(0, 0, dz, dy)),
            device_id_type=MESH,
        )

    for dx in (1, 2, 3):
        f1_copy(dx).start()
    f1[x] = fsrc[pl.ds(x * 8, 8)]

    def drain(g, carry):
        for t in range(2):
            for i in (1, 2, 3):
                send1(t, g, i, 0).wait_send()

        return carry

    lax.fori_loop(0, 4, drain, 0)
    for t in range(2):
        for g in (1, 2, 3):
            send2(t, g).wait_send()
    send3.wait_send()
    for dx in (1, 2, 3):
        f1_copy(dx).wait_recv()
    for dz, dy in plane:
        f2_copy(dz, dy).start()
    fin[:, z * 4 + y] = f1[:, z * 4 + y]
    for dz, dy in plane:
        f2_copy(dz, dy).wait_recv()

    for dx in (1, 2, 3):
        f1_copy(dx).wait_send()
    for dz, dy in plane:
        f2_copy(dz, dy).wait_send()


def per_device(visibilities, coherencies, flags, freedom, gains):
    own = jnp.transpose(gains, (1, 2, 3, 0)).reshape(128, 4, 32)
    vmem = pl.BlockSpec(memory_space=pltpu.VMEM)
    hbm = pl.BlockSpec(memory_space=pl.ANY)
    dma = pltpu.SemaphoreType.DMA
    slab = (192, 128)
    fin = pl.pallas_call(
        kernel,
        out_shape=jax.ShapeDtypeStruct((4, 8, 4, 128), F32),
        in_specs=[hbm, hbm, hbm, vmem, vmem],
        out_specs=vmem,
        scratch_shapes=[
            pltpu.VMEM((32, 16, 8, 16, 128), BF16),
            pltpu.VMEM((32, 8, 16, 128), BF16),
            pltpu.VMEM((32, 16, 128), jnp.int32),
            pltpu.VMEM((2, 4, 4, 4, 2, 4, 4, 128), F32),
            pltpu.VMEM((2, 4, 4, 4, 4, 128), F32),
            pltpu.VMEM((3, 64, 128), F32),
            pltpu.VMEM((6, 16, 128), F32),
            pltpu.VMEM((16, 12, 16, 128), F32),
            pltpu.VMEM((13, 16, 128), F32),
            pltpu.VMEM((1536, 128), F32),
            pltpu.VMEM((16, 128), F32),
            pltpu.VMEM((2, 128, 128), F32),
            pltpu.VMEM((32,) + slab, F32),
            pltpu.VMEM((2, 4, 3) + slab, F32),
            pltpu.VMEM((2, 4) + slab, F32),
            pltpu.VMEM((2, 3) + slab, F32),
            pltpu.VMEM((2,) + slab, F32),
            pltpu.VMEM(slab, F32),
            pltpu.VMEM((32, 4, 128), F32),
            pltpu.VMEM((4, 8, 4, 128), F32),
            pltpu.VMEM((2, 4, 4, 4, 128), F32),
            dma((34,)),
            dma((64,)), dma((64,)),
            dma((32,)), dma((32,)),
            dma((32,)), dma((32,)),
            dma((32,)), dma((32,)),
            dma((8,)), dma((8,)),
            dma, dma,
            dma((4,)), dma((4,)),
            dma((8,)), dma((8,)),
        ],
        compiler_params=pltpu.CompilerParams(
            collective_id=0, has_side_effects=True, vmem_limit_bytes=56 * 2**20
        ),
        cost_estimate=pl.CostEstimate(flops=10**9, bytes_accessed=2 * 10**7, transcendentals=0),
    )(
        visibilities.reshape(32, 8, 16, 128),
        coherencies.reshape(32, 16, 8, 16, 128),
        flags.reshape(32, 16, 128),
        freedom.reshape(4, 128),
        own,
    )
    return jnp.transpose(fin.reshape(32, 4, 8, 16), (0, 2, 3, 1))


def solution(mesh):
    return jax.shard_map(
        per_device,
        mesh=mesh,
        in_specs=(
            P(None, None, None, "col", "row"),
            P(None, None, None, None, "col", "row"),
            P(None, None, "col", "row"),
            P(),
            P(None, None, None, ("row", "col")),
        ),
        out_specs=P(None, None, None, ("row", "col")),
        check_vma=False,
    )
```

```python
import jax
import jax.numpy as jnp
from jax import lax
from jax.experimental import pallas as pl
from jax.experimental.pallas import tpu as pltpu
from jax.sharding import PartitionSpec as P

F32 = jnp.float32
BF16 = jnp.bfloat16
MESH = pl.DeviceIdType.MESH
damping = 1.0


def product(a, b):
    out = [None] * 8
    for i in range(2):
        for j in range(2):
            real = (
                a[2 * i] * b[j]
                - a[4 + 2 * i] * b[4 + j]
                + a[2 * i + 1] * b[2 + j]
                - a[5 + 2 * i] * b[6 + j]
            )
            imag = (
                a[2 * i] * b[4 + j]
                + a[4 + 2 * i] * b[j]
                + a[2 * i + 1] * b[6 + j]
                + a[5 + 2 * i] * b[2 + j]
            )
            out[2 * i + j] = real
            out[4 + 2 * i + j] = imag
    return out


def prepare_gains(g, gq, gv, tab):
    a = g[:64]
    b = g[64:]
    gv[0] = a
    gv[1] = a + b
    gv[2] = b - a
    r = jnp.concatenate([gq] * 8, axis=0).T
    lane = lax.broadcasted_iota(jnp.int32, (16, 128), 1)
    sec = (lane // 16) % 4
    low = lane >= 64

    def pick(u0, u1, u2, u3):
        return jnp.where(sec == 0, u0, jnp.where(sec == 1, u1, jnp.where(sec == 2, u2, u3)))

    for j in range(2):
        r0, r1, i0, i1 = (r[m * 16 : m * 16 + 16] for m in (2 * j, 2 * j + 1, 4 + 2 * j, 5 + 2 * j))
        rows = [pick(r0, r1, i0, i1), pick(-i0, -i1, r0, r1), pick(r0 - i0, r1 - i1, i0 + r0, i1 + r1)]
        for v in range(3):
            hi = rows[v].astype(BF16).astype(F32)
            tab[j * 3 + v] = jnp.where(low, rows[v] - hi, hi)


def channel_sums(coh, vis, flag, nu, gv, tab, ys, wr, red, slab):
    lane = lax.broadcasted_iota(jnp.int32, (16, 128), 1)
    line = lax.broadcasted_iota(jnp.int32, (16, 128), 0)
    diag = (lane % 16) == line
    acc = [[jnp.zeros((16, 128), F32) for _ in range(3)] for _ in range(4)]
    for k in range(16):
        lhs = jnp.concatenate([jnp.where(diag, tab[g, k : k + 1, :], 0.0) for g in range(6)], axis=0).astype(BF16)
        half = jnp.concatenate(
            [
                jnp.concatenate([coh[k, 4 * ri + l], coh[k, 4 * ri + 2 + l]], axis=1)
                for ri in range(2)
                for l in range(2)
            ],
            axis=0,
        )
        out = jnp.dot(lhs, jnp.concatenate([half, half], axis=0), preferred_element_type=F32)
        y = {}
        for i in range(2):
            for j in range(2):
                for v in range(3):
                    t = out[(j * 3 + v) * 16 : (j * 3 + v) * 16 + 16, i * 128 : i * 128 + 128]
                    y[i, j, v] = t
                    ys[k, (i * 2 + j) * 3 + v] = t
        for i in range(2):
            for j in range(2):
                for l in range(2):
                    at = (2 * i + l) * 16 + k
                    ga, gs, gd = (gv[v, at : at + 1, :] for v in range(3))
                    part = acc[2 * i + j]
                    part[0] = part[0] + ga * y[l, j, 2]
                    part[1] = part[1] + gs * y[l, j, 1]
                    part[2] = part[2] + gd * y[l, j, 0]
    resid = []
    energy = None
    for m in range(4):
        re = vis[m].astype(F32) - (acc[m][0] - acc[m][1])
        im = vis[4 + m].astype(F32) - (acc[m][0] + acc[m][2])
        resid.append((re, im))
        t = re * re + im * im
        energy = t if energy is None else energy + t
    w = flag.astype(F32) * (nu + 8.0) / (nu + energy)
    for m in range(4):
        a = w * resid[m][0]
        b = w * resid[m][1]
        wr[m * 3] = a
        wr[m * 3 + 1] = a - b
        wr[m * 3 + 2] = a + b
    wr[12] = w
    for k in range(16):
        tot = [None] * 12
        cross = [[None] * 3 for _ in range(4)]
        for h in range(2):
            s = slice(8 * h, 8 * h + 8)
            y = [[[ys[k, (i * 2 + j) * 3 + v, s] for v in range(3)] for j in range(2)] for i in range(2)]
            for i in range(2):
                for j in range(2):
                    for l in range(2):
                        yr, yi, both = y[j][l]
                        at = (2 * i + l) * 3
                        terms = (wr[at, s] * both, wr[at + 1, s] * yi, wr[at + 2, s] * yr)
                        part = cross[2 * i + j]
                        for v in range(3):
                            part[v] = terms[v] if part[v] is None else part[v] + terms[v]
            (r00, i00, _), (r01, i01, _) = y[0]
            (r10, i10, _), (r11, i11, _) = y[1]
            every = (
                r00 * r00 + i00 * i00 + r01 * r01 + i01 * i01,
                r10 * r10 + i10 * i10 + r11 * r11 + i11 * i11,
                r00 * r10 + i00 * i10 + r01 * r11 + i01 * i11,
                i00 * r10 - r00 * i10 + i01 * r11 - r01 * i11,
            )
            for t in range(4):
                x = wr[12, s] * every[t]
                tot[8 + t] = x if h == 0 else tot[8 + t] + x
        for m in range(4):
            tot[m] = cross[m][0] - cross[m][1]
            tot[4 + m] = cross[m][2] - cross[m][0]
        for t in range(12):
            red[pl.ds((t * 16 + k) * 8, 8), :] = tot[t]
    for b in range(24):
        s = None
        for j in range(8):
            x = red[pl.ds(b * 64 + j, 8, stride=8), :]
            s = x if s is None else s + x
        slab[pl.ds(b * 8, 8), :] = s


def updated(g, total):
    share = [total[t * 16 : t * 16 + 16] for t in range(12)]
    upper_a = share[8] + damping
    lower_d = share[9] + damping
    part_re = share[10]
    part_im = share[11]
    determ = upper_a * lower_d - part_re * part_re - part_im * part_im
    zeros = jnp.zeros_like(upper_a)
    inverse = [
        lower_d / determ,
        -part_re / determ,
        -part_re / determ,
        upper_a / determ,
        zeros,
        -part_im / determ,
        part_im / determ,
        zeros,
    ]
    return g + jnp.concatenate(product(share[:8], inverse), axis=0)


def kernel(
    vis_hbm, coh_hbm, flag_hbm, free_ref, own_ref, fin,
    coh_v, vis_v, flag_v, ag, gqb, gv, tab, ys, wr, red, nu_v, gsv,
    slabs, r1, p1, r2, p2, r3, fsrc, f1,
    gl, load_sem, s1_send, s1_recv, gq_send, gq_recv, s3_send, s3_recv,
    p1_send, p1_recv, p2_send, p2_recv, p3_send, p3_recv, f1_send, f1_recv, f2_send, f2_recv,
):
    row = lax.axis_index("row")
    col = lax.axis_index("col")
    x = col // 8
    z = (col // 4) % 2
    y = col % 4

    def col_of(xx, zz, yy):
        return xx * 8 + zz * 4 + yy

    def moved(t, da, dz, db):
        return col_of((x + (1 - t) * da + t * db) % 4, (z + dz) % 2, (y + t * da + (1 - t) * db) % 4)

    def axis_a(t):
        return x + t * (y - x)

    def axis_b(t):
        return y + t * (x - y)

    def relay_side(t, g):
        return 1 + 2 * ((t + g) % 2)

    lead = 4

    def flag_of(cond):
        return cond.astype(jnp.int32)

    def step(n):
        m = n - lead
        first = flag_of(n < lead)
        last = flag_of(n >= 32 - lead)
        between = (1 - first) * (1 - last)
        mine = last + between * (1 - m % 2)
        j = first * n + last * (n - 16) + between * (m // 2 + (m % 2) * lead)
        t = mine * z + (1 - mine) * (1 - z)
        g = (j // 4 + 1) % 4
        i = j % 4
        d = relay_side(t, g)
        s = 2 * flag_of(i == 0) + (4 - d) * flag_of(i == 1) + d * flag_of(i == 2)
        alpha = (axis_a(t) + s) % 4
        beta = (axis_b(t) + g) % 4
        return t, j, g, s, alpha, beta

    def channel_of(t, alpha, beta):
        return (1 - t) * (alpha * 8 + beta) + t * (beta * 8 + 4 + alpha)

    def load(n):
        t, _, _, _, alpha, beta = step(n)
        return pltpu.make_async_copy(coh_hbm.at[channel_of(t, alpha, beta)], coh_v.at[n], load_sem.at[n])

    vis_copy = pltpu.make_async_copy(vis_hbm, vis_v, load_sem.at[32])
    flag_copy = pltpu.make_async_copy(flag_hbm, flag_v, load_sem.at[33])

    gq_target = (y, col_of(row, x // 2, (x % 2) * 2 + z))
    gq_source = (x, col_of(z * 2 + y // 2, y % 2, row))
    gq_far = jnp.logical_or(gq_target[0] != row, gq_target[1] != col)
    gq_from_far = jnp.logical_or(gq_source[0] != row, gq_source[1] != col)

    peers = [moved(0, da, 0, 0) for da in (1, 2, 3)]
    peers += [moved(0, 0, dz, db) for dz in range(2) for db in range(4) if (dz, db) != (0, 0)]
    peers += [moved(0, da, 1, 0) for da in (1, 2, 3)]
    barrier = pltpu.get_barrier_semaphore()
    for peer in peers:
        pl.semaphore_signal(barrier, inc=1, device_id=(row, peer), device_id_type=MESH)
    for dr in (1, 2, 3):
        pl.semaphore_signal(barrier, inc=1, device_id=((row + dr) % 4, col), device_id_type=MESH)

    @pl.when(gq_from_far)
    def _():
        pl.semaphore_signal(barrier, inc=1, device_id=gq_source, device_id_type=MESH)

    lax.fori_loop(0, 2, lambda n, u: (load(n).start(), u)[1], 0)
    vis_copy.start()
    flag_copy.start()
    lax.fori_loop(2, 32, lambda n, u: (load(n).start(), u)[1], 0)

    turned = jnp.concatenate([own_ref[:, p, :] for p in range(4)], axis=1).T
    for p in range(4):
        for cx in range(4):
            for cy in range(4):
                for t, beta, alpha in ((0, cy, cx), (1, cx, cy)):
                    at = p * 32 + cx * 8 + t * 4 + cy
                    gl[t, beta, alpha, p : p + 1] = turned[at : at + 1]
    for t in range(2):
        ag[t, :, :, x, z, y] = gl[t]

    @pl.when(jnp.logical_not(gq_from_far))
    def _():
        for t in range(2):
            gqb[t, :, :, row] = gl[t]

    lane = lax.broadcasted_iota(jnp.int32, (16, 128), 1)
    line = lax.broadcasted_iota(jnp.int32, (16, 128), 0)
    free_q = jnp.broadcast_to(free_ref[pl.ds(x, 1), :].astype(F32), (16, 128))
    free_q = jnp.sum(jnp.where(lane == (z * 4 + y) * 16 + line, free_q, 0.0), axis=1, keepdims=True)
    nu_v[...] = free_q + free_ref[pl.ds(row, 1), :].astype(F32)

    pl.semaphore_wait(barrier, 16 + gq_far.astype(jnp.int32))

    def s1(t, g, dz, db):
        beta = (axis_b(t) + db + g) % 4
        at = t * 32 + g * 8 + dz * 4 + db
        return pltpu.make_async_remote_copy(
            src_ref=gl.at[t, beta],
            dst_ref=ag.at[t, beta, :, x, z, y],
            send_sem=s1_send.at[at],
            recv_sem=s1_recv.at[at],
            device_id=(row, moved(t, 0, dz, db)),
            device_id_type=MESH,
        )

    def gq_copy(t, g):
        second = (1 - t) * ((x % 2) * 2 + z) + t * row
        beta = (second + g) % 4
        return pltpu.make_async_remote_copy(
            src_ref=gl.at[t, beta],
            dst_ref=gqb.at[t, beta, :, y],
            send_sem=gq_send.at[t * 16 + g * 4],
            recv_sem=gq_recv.at[t * 16 + g * 4],
            device_id=gq_target,
            device_id_type=MESH,
        )

    def gq_arrival(t, g):
        beta = (axis_b(t) + g) % 4
        return pltpu.make_async_remote_copy(
            src_ref=gl.at[t, beta],
            dst_ref=gqb.at[t, beta, :, row],
            send_sem=gq_send.at[t * 16 + g * 4],
            recv_sem=gq_recv.at[t * 16 + g * 4],
            device_id=gq_target,
            device_id_type=MESH,
        )

    def gq_row_copy(t, g, dr):
        beta = (axis_b(t) + g) % 4
        block = gqb.at[t, beta, :, row]
        return pltpu.make_async_remote_copy(
            src_ref=block,
            dst_ref=block,
            send_sem=gq_send.at[t * 16 + g * 4 + dr],
            recv_sem=gq_recv.at[t * 16 + g * 4 + dr],
            device_id=((row + dr) % 4, col),
            device_id_type=MESH,
        )

    def gq_row_arrival(t, g, dr):
        beta = (axis_b(t) + g) % 4
        return pltpu.make_async_remote_copy(
            src_ref=gl.at[t, beta],
            dst_ref=gqb.at[t, beta, :, (row + 4 - dr) % 4],
            send_sem=gq_send.at[t * 16 + g * 4 + dr],
            recv_sem=gq_recv.at[t * 16 + g * 4 + dr],
            device_id=((row + dr) % 4, col),
            device_id_type=MESH,
        )

    def s3(t, g, s):
        at = t * 16 + g * 4 + s
        beta = (axis_b(t) + g) % 4
        block = ag.at[0, beta, :, x] if t == 0 else ag.at[1, beta, :, :, :, y]
        return pltpu.make_async_remote_copy(
            src_ref=block,
            dst_ref=block,
            send_sem=s3_send.at[at],
            recv_sem=s3_recv.at[at],
            device_id=(row, moved(t, s, 0, 0)),
            device_id_type=MESH,
        )

    plane = [(dz, db) for dz in range(2) for db in range(4) if (dz, db) != (0, 0)]

    def by_type(t, act):
        for tt in range(2):
            @pl.when(t == tt)
            def _():
                act(tt)

    def start_own(t, g):
        for dz, db in plane:
            s1(t, g, dz, db).start()

        @pl.when(gq_far)
        def _():
            gq_copy(t, g).start()

    def forward(t, g):
        for dz, db in plane:
            s1(t, g, dz, db).wait_recv()
        for s in (1, 2, 3):
            s3(t, g, s).start()

        @pl.when(gq_from_far)
        def _():
            gq_arrival(t, g).wait_recv()

        for dr in (1, 2, 3):
            gq_row_copy(t, g, dr).start()

    kept = z
    given = 1 - z
    start_own(0, 1)
    start_own(1, 1)
    by_type(given, lambda t: forward(t, 1))
    start_own(0, 2)
    start_own(1, 2)
    by_type(kept, lambda t: forward(t, 1))
    vis_copy.wait()
    flag_copy.wait()

    def send1(t, g, s, j):
        at = t * 16 + g * 4 + s
        return pltpu.make_async_remote_copy(
            src_ref=slabs.at[t * 16 + j],
            dst_ref=r1.at[t, g, s - 1],
            send_sem=p1_send.at[at],
            recv_sem=p1_recv.at[at],
            device_id=(row, moved(t, s, 0, 0)),
            device_id_type=MESH,
        )

    def send2(t, g):
        at = t * 4 + g
        return pltpu.make_async_remote_copy(
            src_ref=p1.at[t, g],
            dst_ref=r2.at[t, g - 1],
            send_sem=p2_send.at[at],
            recv_sem=p2_recv.at[at],
            device_id=(row, moved(t, 0, 0, g)),
            device_id_type=MESH,
        )

    send3 = pltpu.make_async_remote_copy(
        src_ref=p2.at[1 - z],
        dst_ref=r3,
        send_sem=p3_send,
        recv_sem=p3_recv,
        device_id=(row, moved(0, 0, 1, 0)),
        device_id_type=MESH,
    )

    def sum1(t, g, j):
        for i in (1, 2, 3):
            send1(t, g, i, 0).wait_recv()
        p1[t, g] = slabs[t * 16 + j] + r1[t, g, 0] + r1[t, g, 1] + r1[t, g, 2]

    def sum2(t):
        sum1(t, 0, 15)
        for g in (1, 2, 3):
            send2(t, g).wait_recv()
        p2[t] = p1[t, 0] + r2[t, 0] + r2[t, 1] + r2[t, 2]

    def body(n, carry):
        t, j, g, s, alpha, beta = step(n)
        i = j % 4
        load(n).wait()

        def at(*steps):
            hit = n == steps[0]
            for other in steps[1:]:
                hit = jnp.logical_or(hit, n == other)
            return pl.when(hit)

        @at(0, 6, 14)
        def _():
            by_type(given, lambda tt: forward(tt, (2 + flag_of(n >= 6) + flag_of(n >= 14)) % 4))

        @at(5, 13, 21)
        def _():
            by_type(kept, lambda tt: forward(tt, (2 + flag_of(n >= 13) + flag_of(n >= 21)) % 4))

        @at(1, 8)
        def _():
            for tt in range(2):
                start_own(tt, (3 + flag_of(n >= 8)) % 4)

        for tt in range(2):
            @pl.when(jnp.logical_and(i == 0, t == tt))
            def _():
                for k in (1, 2, 3):
                    s3(tt, g, k).wait_recv()
                    gq_row_arrival(tt, g, k).wait_recv()

        gains = ag[t, beta, alpha].reshape(128, 128).T
        prepare_gains(gains, gqb[t, beta, alpha].reshape(16, 128), gv, tab)

        @pl.when(j == 15)
        def _():
            gsv[t] = gains

        c = channel_of(t, alpha, beta)
        channel_sums(
            coh_v.at[n], vis_v.at[c], flag_v[c], nu_v[...], gv, tab, ys, wr, red, slabs.at[t * 16 + j]
        )

        @pl.when(i != 3)
        def _():
            send1(t, g, s, j).start()

        @pl.when(jnp.logical_and(i == 1, j > 4))
        def _():
            sum1(t, j // 4, (j // 4) * 4 - 1)
            send2(t, j // 4).start()

        @pl.when(n == 29)
        def _():
            sum2(given)
            send3.start()

        return carry

    lax.fori_loop(0, 32, body, 0)

    def drain_gains(g, carry):
        for t in range(2):
            for dz, db in plane:
                s1(t, g, dz, db).wait_send()
            for s in (1, 2, 3):
                s3(t, g, s).wait_send()
            for dr in (1, 2, 3):
                gq_row_copy(t, g, dr).wait_send()

            @pl.when(gq_far)
            def _():
                gq_copy(t, g).wait_send()

        return carry

    lax.fori_loop(0, 4, drain_gains, 0)

    sum2(kept)
    send3.wait_recv()
    fresh = updated(gsv[z], p2[z] + r3[...]).T
    for d in range(32):
        fsrc[d] = fresh[d * 4 : d * 4 + 4]

    def f1_copy(dx):
        return pltpu.make_async_remote_copy(
            src_ref=fsrc.at[pl.ds(((x + dx) % 4) * 8, 8)],
            dst_ref=f1.at[x],
            send_sem=f1_send.at[dx],
            recv_sem=f1_recv.at[dx],
            device_id=(row, moved(0, dx, 0, 0)),
            device_id_type=MESH,
        )

    def f2_copy(dz, dy):
        zz = (z + dz) % 2
        yy = (y + dy) % 4
        return pltpu.make_async_remote_copy(
            src_ref=f1.at[:, zz * 4 + yy],
            dst_ref=fin.at[:, z * 4 + y],
            send_sem=f2_send.at[dz * 4 + dy],
            recv_sem=f2_recv.at[dz * 4 + dy],
            device_id=(row, moved(0, 0, dz, dy)),
            device_id_type=MESH,
        )

    for dx in (1, 2, 3):
        f1_copy(dx).start()
    f1[x] = fsrc[pl.ds(x * 8, 8)]

    def drain(g, carry):
        for t in range(2):
            for i in (1, 2, 3):
                send1(t, g, i, 0).wait_send()

        return carry

    lax.fori_loop(0, 4, drain, 0)
    for t in range(2):
        for g in (1, 2, 3):
            send2(t, g).wait_send()
    send3.wait_send()
    for dx in (1, 2, 3):
        f1_copy(dx).wait_recv()
    for dz, dy in plane:
        f2_copy(dz, dy).start()
    fin[:, z * 4 + y] = f1[:, z * 4 + y]
    for dz, dy in plane:
        f2_copy(dz, dy).wait_recv()

    for dx in (1, 2, 3):
        f1_copy(dx).wait_send()
    for dz, dy in plane:
        f2_copy(dz, dy).wait_send()


def per_device(visibilities, coherencies, flags, freedom, gains):
    own = jnp.transpose(gains, (1, 2, 3, 0)).reshape(128, 4, 32)
    vmem = pl.BlockSpec(memory_space=pltpu.VMEM)
    hbm = pl.BlockSpec(memory_space=pl.ANY)
    dma = pltpu.SemaphoreType.DMA
    slab = (192, 128)
    fin = pl.pallas_call(
        kernel,
        out_shape=jax.ShapeDtypeStruct((4, 8, 4, 128), F32),
        in_specs=[hbm, hbm, hbm, vmem, vmem],
        out_specs=vmem,
        scratch_shapes=[
            pltpu.VMEM((32, 16, 8, 16, 128), BF16),
            pltpu.VMEM((32, 8, 16, 128), BF16),
            pltpu.VMEM((32, 16, 128), jnp.int32),
            pltpu.VMEM((2, 4, 4, 4, 2, 4, 4, 128), F32),
            pltpu.VMEM((2, 4, 4, 4, 4, 128), F32),
            pltpu.VMEM((3, 64, 128), F32),
            pltpu.VMEM((6, 16, 128), F32),
            pltpu.VMEM((16, 12, 16, 128), F32),
            pltpu.VMEM((13, 16, 128), F32),
            pltpu.VMEM((1536, 128), F32),
            pltpu.VMEM((16, 128), F32),
            pltpu.VMEM((2, 128, 128), F32),
            pltpu.VMEM((32,) + slab, F32),
            pltpu.VMEM((2, 4, 3) + slab, F32),
            pltpu.VMEM((2, 4) + slab, F32),
            pltpu.VMEM((2, 3) + slab, F32),
            pltpu.VMEM((2,) + slab, F32),
            pltpu.VMEM(slab, F32),
            pltpu.VMEM((32, 4, 128), F32),
            pltpu.VMEM((4, 8, 4, 128), F32),
            pltpu.VMEM((2, 4, 4, 4, 128), F32),
            dma((34,)),
            dma((64,)), dma((64,)),
            dma((32,)), dma((32,)),
            dma((32,)), dma((32,)),
            dma((32,)), dma((32,)),
            dma((8,)), dma((8,)),
            dma, dma,
            dma((4,)), dma((4,)),
            dma((8,)), dma((8,)),
        ],
        compiler_params=pltpu.CompilerParams(
            collective_id=0, has_side_effects=True, vmem_limit_bytes=56 * 2**20
        ),
        cost_estimate=pl.CostEstimate(flops=10**9, bytes_accessed=2 * 10**7, transcendentals=0),
    )(
        visibilities.reshape(32, 8, 16, 128),
        coherencies.reshape(32, 16, 8, 16, 128),
        flags.reshape(32, 16, 128),
        freedom.reshape(4, 128),
        own,
    )
    return jnp.transpose(fin.reshape(32, 4, 8, 16), (0, 2, 3, 1))


def solution(mesh):
    return jax.shard_map(
        per_device,
        mesh=mesh,
        in_specs=(
            P(None, None, None, "col", "row"),
            P(None, None, None, None, "col", "row"),
            P(None, None, "col", "row"),
            P(),
            P(None, None, None, ("row", "col")),
        ),
        out_specs=P(None, None, None, ("row", "col")),
        check_vma=False,
    )
```
